768 devices in a mesh: grp: 64 (over y, x, core), mem: 12 (over z).
Axes of the slice: x: 4, y: 8, z: 12, core: 2. Of those that a mesh axis runs over, the one named last changes fastest.
Arguments:
- dyn_state: float32 [2, 58, 256, 384], P(None, None, 'grp', 'mem'), may hold values from -6 to 6
- wind_speed: float32 [58, 256, 384], P(None, 'grp', 'mem'), may hold values from -4 to 4
- mass_weight: float32 [256, 384], P('grp', 'mem'), may hold values from 0.5 to 2
- crm_state: float32 [24576, 58, 128], P(('grp', 'mem')), may hold values from -6 to 6
- batch_map: int32 [24576], P(('grp', 'mem')), may hold values from 0 to 383, as said below
- sub_steps: int32 [24576], P(('grp', 'mem')), may hold values from 1 to 2
- migrate_to: int32 [24576], P(('grp', 'mem')), may hold values from 0 to 24575, as said below
Outputs:
- dyn_next: float32 [2, 58, 256, 384], P(None, None, 'grp', 'mem')
- phys_tend: float32 [2, 58, 24576], P(None, None, ('grp', 'mem'))
- crm_next: float32 [24576, 58, 128], P(('grp', 'mem'))
The draws below stay inside these ranges and needn't reach their ends.
Inputs may be any that keep to these rules, and one draw needn't show every extreme that they name: `batch_map`: within each aligned block of 384 slots (one group), the entries are a permutation of 0 to 383. `migrate_to`: A permutation of all slots. Every slot goes to a device with the same mem index. Exactly 32 of one device's slots leave its group, at most one of them to any one other device; the rest move within the device.
All inputs are finite; a program needn't handle non-finite values.
Results may differ from the reference program's by a relative error of at most 0.0003.
Values sent between devices are 32-bit elements; how exact they have to be, the bound alone decides.
No kernel may reach another device: no remote copies, remote signals or barrier semaphores. Data moves between devices by JAX's collectives and lax.ppermute only.
A program may use at most 64 MiB of HBM per device.

```python
import math
import jax
import jax.numpy as jnp
import numpy as np
from jax import lax

LEV = 58
CRMX = 64
NSUB = 2
EX = 8
PCOL = 32
GROUP_COLS = 384
COLUMNS = 24576
GY = 256
GX = 384
MOVES = 32
N_GRP = 64
N_MEM = 12
DEVICES = 768


def draw_batch_map(key, part):
    group_keys = jax.random.split(jax.random.fold_in(key, 11), N_GRP)
    orders = jax.vmap(lambda single_column: jax.random.permutation(single_column, GROUP_COLS))(group_keys)
    return orders.reshape(-1).astype(jnp.int32)


def draw_migrate_to(key, part):
    base = jax.random.fold_in(key, 23)

    def one_column(member):
        member_key = jax.random.fold_in(base, member)
        first_key, second_key, third_key = jax.random.split(member_key, 3)
        shifts = jax.random.permutation(first_key, N_GRP - 1)[:MOVES] + 1
        chosen = jax.random.permutation(second_key, PCOL)[:MOVES]
        shift_of_slot = jnp.zeros((PCOL,), jnp.int32).at[chosen].set(shifts.astype(jnp.int32))
        group_index = jnp.arange(N_GRP, dtype=jnp.int32)[:, None]
        dest_group = (group_index + shift_of_slot[None, :]) % N_GRP
        orders = jax.vmap(lambda single_column: jax.random.permutation(single_column, PCOL))(jax.random.split(third_key, N_GRP)).astype(jnp.int32)
        slot_index = jnp.broadcast_to(jnp.arange(PCOL, dtype=jnp.int32)[None, :], (N_GRP, PCOL))
        dest_slot = orders[dest_group, slot_index]
        return (dest_group * N_MEM + member) * PCOL + dest_slot
    every = jax.vmap(one_column)(jnp.arange(N_MEM, dtype=jnp.int32))
    return every.transpose(1, 0, 2).reshape(-1).astype(jnp.int32)


def with_ends(values, stream_key, low, top_value):
    dims = values.shape
    index_at = [jax.random.randint(jax.random.fold_in(stream_key, axis), (), 0, dims[axis]) for axis in range(len(dims))]
    values = values.at[tuple(index_at)].set(low)
    longest = dims.index(max(dims))
    index_at[longest] = (index_at[longest] + 1) % dims[longest]
    return values.at[tuple(index_at)].set(top_value)


def block_scale(own_key, extent, cuts, low, largest):
    gain, own = 1.0, jax.random.fold_in(own_key, 6)
    for dim, blocks in cuts:
        heights = jnp.exp(jax.random.uniform(jax.random.fold_in(own, dim), (blocks,), jnp.float32, low / len(cuts), largest / len(cuts)))
        gain = gain * jnp.repeat(heights, extent[dim] // blocks).reshape([-1 if axis == dim else 1 for axis in range(len(extent))])
    return gain


def scatter_about(key, shape, scale, reach, pieces=(), kind=jnp.bfloat16):
    values = scale * jax.random.normal(key, shape, jnp.float32)
    if pieces:
        values = values * block_scale(key, shape, pieces, -0.22, 0.18)
    return jnp.clip(values, -reach, reach).astype(kind)


def setup_inputs(seed: int = 0) -> dict:
    key_of = jax.random.split(jax.random.key(seed), 8)
    dyn_state = scatter_about(key_of[0], (2, LEV, GY, GX), 1.0, 6.0, ((2, 64), (3, 12)), jnp.float32)
    wind_speed = scatter_about(key_of[1], (LEV, GY, GX), 1.0, 4.0, ((1, 64), (2, 12)), jnp.float32)
    mass_weight = jnp.clip(jnp.exp(math.log(2.0) - 1.3862944 * jax.random.uniform(key_of[2], (GY, GX), jnp.float32) ** block_scale(key_of[2], (GY, GX), ((0, 64), (1, 12)), -0.2, 0.2)), 0.5, 2.0)
    crm_state = scatter_about(key_of[3], (COLUMNS, LEV, 2 * CRMX), 1.0, 6.0, ((0, 768),), jnp.float32)
    batch_map = draw_batch_map(jax.random.fold_in(key_of[7], 71), 0)
    sub_steps = with_ends(jax.random.randint(key_of[5], (COLUMNS,), 1, NSUB + 1), jax.random.fold_in(key_of[5], 1), 1, NSUB).astype(jnp.int32)
    migrate_to = draw_migrate_to(jax.random.fold_in(key_of[7], 71), 0)
    return {"dyn_state": dyn_state, "wind_speed": wind_speed, "mass_weight": mass_weight, "crm_state": crm_state, "batch_map": batch_map, "sub_steps": sub_steps, "migrate_to": migrate_to}


def derivative_table():
    nodes = np.array([-1.0, -1.0 / np.sqrt(5.0), 1.0 / np.sqrt(5.0), 1.0])
    table = np.zeros((4, 4))
    for target_node in range(4):
        for source_node in range(4):
            if target_node == source_node:
                table[target_node, source_node] = sum((1.0 / (nodes[source_node] - nodes[other_node]) for other_node in range(4) if other_node != source_node))
            else:
                numerator = 1.0
                for other_node in range(4):
                    if other_node != source_node and other_node != target_node:
                        numerator = numerator * (nodes[target_node] - nodes[other_node])
                denominator = 1.0
                for other_node in range(4):
                    if other_node != source_node:
                        denominator = denominator * (nodes[source_node] - nodes[other_node])
                table[target_node, source_node] = numerator / denominator
    return table.astype(np.float32)

def element_derivative(field):
    shape_in = field.shape
    blocks = field.reshape(shape_in[:-1] + (shape_in[-1] // 4, 4))
    table = jnp.asarray(derivative_table()).astype(field.dtype)
    result = jnp.einsum('...ej,ij->...ei', blocks, table, precision=lax.Precision.HIGHEST)
    return result.reshape(shape_in)

def assemble_axis(values, axis):
    length = values.shape[axis]
    shape_b = [1] * values.ndim
    shape_b[axis] = length
    position = jnp.arange(length, dtype=jnp.int32)
    opening = (position % 4 == 0).reshape(shape_b)
    closing = (position % 4 == 3).reshape(shape_b)
    return values + jnp.where(opening, jnp.roll(values, 1, axis), 0.0) + jnp.where(closing, jnp.roll(values, -1, axis), 0.0)

def second_levels(values):
    upper = jnp.concatenate([values[:, 1:], values[:, -1:]], 1)
    lower = jnp.concatenate([values[:, :1], values[:, :-1]], 1)
    return upper + lower - 2.0 * values

def second_columns(values):
    return jnp.roll(values, 1, -1) + jnp.roll(values, -1, -1) - 2.0 * values

def crm_run(state, forcing, steps):
    width = state.shape[-1] // 2
    force_heat = forcing[0].T[:, :, None]
    force_moist = forcing[1].T[:, :, None]
    thermal = state[..., :width]
    moisture = state[..., width:]
    for substep in range(NSUB):
        condense = 0.1 * jax.nn.softplus(moisture - thermal)
        thermal_new = thermal + 0.25 * force_heat + 0.15 * second_columns(thermal) + 0.1 * second_levels(thermal) + 0.5 * condense
        moisture_new = moisture + 0.25 * force_moist + 0.15 * second_columns(moisture) + 0.1 * second_levels(moisture) - condense
        active = (steps > substep)[:, None, None]
        thermal = jnp.where(active, thermal_new, thermal)
        moisture = jnp.where(active, moisture_new, moisture)
    final = jnp.concatenate([thermal, moisture], -1)
    tendency = jnp.stack([lax.optimization_barrier(jnp.mean(thermal - state[..., :width], -1)).T, lax.optimization_barrier(jnp.mean(moisture - state[..., width:], -1)).T])
    return (final, tendency)

def reference(dyn_state, wind_speed, mass_weight, crm_state, batch_map, sub_steps, migrate_to):
    advection = -wind_speed[None] * element_derivative(dyn_state)
    numerator = assemble_axis(assemble_axis(mass_weight[None, None] * advection, 3), 2)
    denominator = assemble_axis(assemble_axis(mass_weight, 1), 0)
    assembled = numerator / denominator
    dyn_next = dyn_state + 0.2 * assembled
    levels = dyn_state.shape[1]
    blocked = assembled.reshape(2, levels, GY // 2, 2, GX // 2, 2).mean((3, 5))
    blocked = blocked.reshape(2, levels, N_GRP, 2, N_MEM, 2 * EX).transpose(0, 1, 2, 4, 3, 5)
    forcing = blocked.reshape(2, levels, COLUMNS)
    group_base = jnp.arange(COLUMNS, dtype=jnp.int32) // GROUP_COLS * GROUP_COLS
    source = (group_base + batch_map).astype(jnp.int32)
    forcing_position = forcing[:, :, source]
    state_blocks = crm_state.reshape(DEVICES, PCOL, levels, crm_state.shape[-1])
    force_blocks = forcing_position.reshape(2, levels, DEVICES, PCOL).transpose(2, 0, 1, 3)
    step_blocks = sub_steps.reshape(DEVICES, PCOL)

    def per_device(bundle):
        return crm_run(bundle[0], bundle[1], bundle[2])
    stepped, tendency_blocks = lax.map(per_device, (state_blocks, force_blocks, step_blocks))
    stepped = stepped.reshape(crm_state.shape)
    tendency_slot = tendency_blocks.transpose(1, 2, 0, 3).reshape(2, levels, COLUMNS)
    phys_tend = jnp.zeros((2, levels, COLUMNS), jnp.float32).at[:, :, source].set(tendency_slot)
    crm_next = jnp.zeros_like(stepped).at[migrate_to.astype(jnp.int32)].set(stepped)
    return (dyn_next, phys_tend, crm_next)
```

```python
import jax
import jax.numpy as jnp
import numpy as np
from jax import lax
from jax.experimental import pallas as pl
from jax.experimental.pallas import tpu as pltpu
from jax.sharding import PartitionSpec as P

NSUB = 2
LEV = 58
HALF = 64
SLOTS = 32
N_GRP = 64
N_MEM = 12
ROWS = 4
POINTS = 32
COLS = SLOTS * N_MEM
HIGH = lax.Precision.HIGHEST
VMEM = pl.BlockSpec(memory_space=pltpu.VMEM)
SMEM = pl.BlockSpec(memory_space=pltpu.SMEM)
F32 = jnp.float32


def derivative_table():
    nodes = np.array([-1.0, -1.0 / np.sqrt(5.0), 1.0 / np.sqrt(5.0), 1.0])
    table = np.zeros((4, 4))
    for i in range(4):
        for j in range(4):
            if i == j:
                table[i, j] = sum(1.0 / (nodes[j] - nodes[k]) for k in range(4) if k != j)
            else:
                top = np.prod([nodes[i] - nodes[k] for k in range(4) if k not in (i, j)])
                low = np.prod([nodes[j] - nodes[k] for k in range(4) if k != j])
                table[i, j] = top / low
    return table.astype(np.float32)


def iota(shape, dim):
    return lax.broadcasted_iota(jnp.int32, shape, dim)


def dot(a, b):
    return jnp.dot(a, b, precision=HIGH, preferred_element_type=F32)


def dot_t(a, b):
    return lax.dot_general(a, b, (((0,), (0,)), ((), ())), precision=HIGH, preferred_element_type=F32)


def to_column(row):
    n = row.shape[1]
    return jnp.sum(jnp.where(iota((n, n), 0) == iota((n, n), 1), row, 0.0), axis=1, keepdims=True)


def both_kinds(heat, moist):
    gap = jnp.zeros((heat.shape[0], HALF - LEV), F32)
    return jnp.concatenate([heat, gap, moist, gap], axis=1)


def bucket_kernel(migrate, state, out):
    for s in range(SLOTS):
        group = lax.div(migrate[s], COLS)
        out[pl.ds(group * LEV, LEV), :] = state[pl.ds(s, LEV, stride=SLOTS), :]


def weigh_kernel(dyn, wind, mass, table, out):
    field = both_kinds(dyn[0].reshape(ROWS * POINTS, LEV), dyn[1].reshape(ROWS * POINTS, LEV))
    blow = wind[...].reshape(ROWS * POINTS, LEV)
    slope = dot(table[...], field)
    column = jnp.concatenate([to_column(mass[y : y + 1, :]) for y in range(ROWS)], axis=0)
    weighed = column * (-both_kinds(blow, blow) * slope)
    lane = iota((ROWS * POINTS, 2 * HALF), 1)
    out[...] = jnp.where(lane == LEV, column, weighed).reshape(ROWS, POINTS, 2 * HALF)


def assemble_kernel(own, before, after, batch, inner, payload):
    rows = [own[0] + before[0], own[1], own[2], own[3] + after[0]]
    point = iota((POINTS, 2 * HALF), 0)
    means, edges = [], []
    for y, row in enumerate(rows):
        opening = (point % 4 == 0) & (point > 0)
        closing = (point % 4 == 3) & (point < POINTS - 1)
        full = (
            row
            + jnp.where(opening, pltpu.roll(row, 1, 0), 0.0)
            + jnp.where(closing, pltpu.roll(row, POINTS - 1, 0), 0.0)
        )
        ratio = full / full[:, LEV : LEV + 1]
        inner[y] = ratio
        means.append(jnp.where((point == 0) | (point == POINTS - 1), 0.0, ratio))
        edges.append(row)
    col, pt = iota((SLOTS, ROWS * POINTS), 0), iota((SLOTS, ROWS * POINTS), 1)
    inside = (col // 16 == pt // (2 * POINTS)) & (col % 16 == (pt % POINTS) // 2)
    average = jnp.where(inside, 0.25, 0.0).astype(F32)
    forcing = dot(average, jnp.concatenate(means, axis=0))
    left = [row[0:1] for row in edges]
    right = [row[POINTS - 1 : POINTS] for row in edges]
    lane = iota((SLOTS, 2 * HALF), 1)
    forcing = jnp.where(lane == LEV, to_column(batch[...].astype(F32)), forcing)
    payload[...] = jnp.concatenate([forcing] + left + right, axis=0)


def forcing_kernel(gathered, batch, migrate, steps, force, edge):
    rows = []
    for d in range(N_MEM):
        right = gathered[d, SLOTS + ROWS : SLOTS + 2 * ROWS, :]
        left = gathered[(d + 1) % N_MEM, SLOTS : SLOTS + ROWS, :]
        both = right + left
        rows.append(both / both[:, LEV : LEV + 1])
    joined = jnp.concatenate(rows, axis=0)
    edge[...] = joined
    columns = gathered[:, :SLOTS, :].reshape(COLS, 2 * HALF)
    slot = batch[...]
    pick = jnp.where(iota((COLS, SLOTS), 0) == slot, 1.0, 0.0).astype(F32)
    e = iota((N_MEM * ROWS, SLOTS), 0)
    dev, half = e // ROWS, (e % ROWS) // 2
    ahead = jnp.where(dev == N_MEM - 1, 0, dev + 1)
    last = slot == dev * SLOTS + half * 16 + 15
    first = slot == ahead * SLOTS + half * 16
    pick_edge = jnp.where(last, 0.25, 0.0) + jnp.where(first, 0.25, 0.0)
    forced = dot_t(pick, columns) + dot_t(pick_edge, joined)
    place = to_column(migrate[...].astype(F32))
    count = to_column(steps[...].astype(F32))
    lane = iota((SLOTS, 2 * HALF), 1)
    force[...] = jnp.where(lane == LEV, place, jnp.where(lane == LEV + 1, count, forced))


def substep(source, level, quarter, active):
    shape = (SLOTS, 2 * HALF)
    lane = iota(shape, 1)
    at = lambda l: source[pl.ds(pl.multiple_of(l * SLOTS, SLOTS), SLOTS), :]
    current = at(level)
    upper = at(jnp.minimum(level + 1, LEV - 1))
    lower = at(jnp.maximum(level - 1, 0))
    heat = lane < HALF
    other = pltpu.roll(current, HALF, 1)
    gap = jnp.where(heat, other - current, current - other)
    soft = jnp.maximum(gap, 0.0) + jnp.log(1.0 + jnp.exp(-jnp.abs(gap)))
    column = lane & (HALF - 1)
    left = pltpu.roll(jnp.where(column == HALF - 1, other, current), 1, 1)
    right = pltpu.roll(jnp.where(column == 0, other, current), 2 * HALF - 1, 1)
    force = jnp.take_along_axis(quarter, (lane & HALF) + level, axis=1, mode="promise_in_bounds")
    updated = (
        current
        + force
        + 0.15 * (left + right - 2.0 * current)
        + 0.1 * (upper + lower - 2.0 * current)
        + jnp.where(heat, 0.05, -0.1) * soft
    )
    return jnp.where(active, updated, current)


def tendency_kernel(state, force, send, middle):
    shape = (SLOTS, 2 * HALF)
    count = force[:, LEV + 1 : LEV + 2]
    quarter = 0.25 * force[...]

    def first(level, carry):
        at = pl.ds(pl.multiple_of(level * SLOTS, SLOTS), SLOTS)
        middle[at, :] = substep(state, level, quarter, count > 0.5)
        return carry

    lax.fori_loop(0, LEV, first, 0, unroll=2)
    lane = iota(shape, 1)
    heat = lane < HALF

    def second(level, total):
        at = pl.ds(pl.multiple_of(level * SLOTS, SLOTS), SLOTS)
        change = substep(middle, level, quarter, count > 1.5) - state[at, :]
        h = jnp.sum(jnp.where(heat, change, 0.0), axis=1, keepdims=True)
        q = jnp.sum(jnp.where(heat, 0.0, change), axis=1, keepdims=True)
        mean = jnp.where(heat, h, q) * (1.0 / HALF)
        return jnp.where((lane & (HALF - 1)) == level, mean, total)

    send[...] = lax.fori_loop(0, LEV, second, jnp.zeros(shape, F32), unroll=2)


def select_kernel(every, force, origin):
    me = lax.axis_index("grp") * COLS + lax.axis_index("mem") * SLOTS
    place = every[:, LEV : LEV + 1] - me.astype(F32)
    slot = iota((N_GRP * SLOTS, SLOTS), 1).astype(F32)
    pick = jnp.where(place == slot, 1.0, 0.0).astype(F32)
    force[...] = dot_t(pick, every[...])
    group = (iota((N_GRP * SLOTS, SLOTS), 0) // SLOTS).astype(F32)
    origin[...] = jnp.sum(pick * group, axis=0, keepdims=True).astype(jnp.int32)


def arrive_kernel(source, main, force, out, held, middle):
    for j in range(SLOTS):
        held[pl.ds(j, LEV, stride=SLOTS), :] = main[pl.ds(source[0, j] * LEV, LEV), :]
    count = force[:, LEV + 1 : LEV + 2]
    quarter = 0.25 * force[...]

    def first(level, carry):
        at = pl.ds(pl.multiple_of(level * SLOTS, SLOTS), SLOTS)
        middle[at, :] = substep(held, level, quarter, count > 0.5)
        return carry

    lax.fori_loop(0, LEV, first, 0, unroll=2)

    def second(level, carry):
        at = pl.ds(pl.multiple_of(level * SLOTS, SLOTS), SLOTS)
        out[at, :] = substep(middle, level, quarter, count > 1.5)
        return carry

    lax.fori_loop(0, LEV, second, 0, unroll=2)


def next_kernel(dyn, inner, edge, out):
    me = lax.axis_index("mem")
    behind = lax.rem(me + N_MEM - 1, N_MEM)
    for y in range(ROWS):
        point = iota((POINTS, 2 * HALF), 0)
        left = edge[pl.ds(behind * ROWS + y, 1), :]
        right = edge[pl.ds(me * ROWS + y, 1), :]
        ratio = jnp.where(point == 0, left, jnp.where(point == POINTS - 1, right, inner[y]))
        out[0, y] = dyn[0, y] + 0.2 * ratio[:, :LEV]
        out[1, y] = dyn[1, y] + 0.2 * ratio[:, HALF : HALF + LEV]


def column_kernel(tendency, gathered, out):
    serves = gathered[:, :SLOTS, :].reshape(COLS, 2 * HALF)[:, LEV : LEV + 1]
    column = (iota((COLS, SLOTS), 1) + lax.axis_index("mem") * SLOTS).astype(F32)
    pick = jnp.where(serves == column, 1.0, 0.0).astype(F32)
    mine = dot_t(pick, tendency[...])
    out[0] = mine[:, :LEV]
    out[1] = mine[:, HALF : HALF + LEV]


def call(kernel, shapes, specs, scratch=()):
    many = isinstance(shapes, list)
    out = [jax.ShapeDtypeStruct(s, F32) for s in shapes] if many else jax.ShapeDtypeStruct(shapes, F32)
    return pl.pallas_call(
        kernel,
        out_shape=out,
        in_specs=specs,
        out_specs=[VMEM] * len(shapes) if many else VMEM,
        scratch_shapes=[pltpu.VMEM(s, F32) for s in scratch],
        compiler_params=pltpu.CompilerParams(vmem_limit_bytes=24 * 2**20),
    )


def on_device(dyn_state, wind_speed, mass_weight, crm_state, batch_map, sub_steps, migrate_to):
    lanes = 2 * HALF
    dyn = dyn_state.transpose(0, 2, 3, 1)
    wind = wind_speed.transpose(1, 2, 0)
    state = crm_state.transpose(1, 0, 2).reshape(LEV * SLOTS, lanes)
    batch, steps, moves = (a.reshape(1, SLOTS) for a in (batch_map, sub_steps, migrate_to))
    table = jnp.asarray(np.kron(np.eye(ROWS * POINTS // 4), derivative_table()).astype(np.float32))

    buckets = call(bucket_kernel, (N_GRP * LEV, lanes), [SMEM, VMEM])(migrate_to, state)
    main = lax.all_to_all(buckets.reshape(N_GRP, LEV // 2, 2, lanes), "grp", 0, 0, tiled=True)

    weighed = call(weigh_kernel, (ROWS, POINTS, lanes), [VMEM] * 4)(dyn, wind, mass_weight, table)
    up = [(i, (i + 1) % N_GRP) for i in range(N_GRP)]
    down = [(j, i) for i, j in up]
    before = lax.ppermute(weighed[ROWS - 1 :], "grp", up)
    after = lax.ppermute(weighed[:1], "grp", down)
    inner, payload = call(
        assemble_kernel, [(ROWS, POINTS, lanes), (SLOTS + 2 * ROWS, lanes)], [VMEM] * 4
    )(weighed, before, after, batch)
    gathered = lax.all_gather(payload, "mem", axis=0)
    force, edge = call(
        forcing_kernel, [(SLOTS, lanes), (N_MEM * ROWS, lanes)], [VMEM] * 4
    )(gathered, batch, moves, steps)
    every = lax.all_gather(force, "grp", axis=0, tiled=True)
    cells = LEV * SLOTS
    tendency = call(tendency_kernel, (SLOTS, lanes), [VMEM] * 2, [(cells, lanes)])(state, force)
    tendencies = lax.all_gather(tendency, "mem", axis=0, tiled=True)
    dyn_next = call(next_kernel, (2, ROWS, POINTS, LEV), [VMEM] * 3)(dyn, inner, edge)
    phys = call(column_kernel, (2, SLOTS, LEV), [VMEM] * 2)(tendencies, gathered)

    brought, origin = pl.pallas_call(
        select_kernel,
        out_shape=[jax.ShapeDtypeStruct((SLOTS, lanes), F32), jax.ShapeDtypeStruct((1, SLOTS), jnp.int32)],
        in_specs=[VMEM],
        out_specs=[VMEM] * 2,
        compiler_params=pltpu.CompilerParams(vmem_limit_bytes=24 * 2**20),
    )(every)
    new = call(arrive_kernel, (cells, lanes), [SMEM, VMEM, VMEM], [(cells, lanes)] * 2)(
        origin, main.reshape(N_GRP * LEV, lanes), brought
    )
    crm_next = new.reshape(LEV, SLOTS, lanes).transpose(1, 0, 2)
    return (dyn_next.transpose(0, 3, 1, 2), phys.transpose(0, 2, 1), crm_next)


def solution(mesh):
    placed = (
        P(None, None, "grp", "mem"),
        P(None, "grp", "mem"),
        P("grp", "mem"),
        P(("grp", "mem"), None, None),
        P(("grp", "mem")),
        P(("grp", "mem")),
        P(("grp", "mem")),
    )
    return jax.shard_map(
        on_device,
        mesh=mesh,
        in_specs=placed,
        out_specs=(
            P(None, None, "grp", "mem"),
            P(None, None, ("grp", "mem")),
            P(("grp", "mem"), None, None),
        ),
        check_vma=False,
    )
```

```python
import jax
import jax.numpy as jnp
import numpy as np
from jax import lax
from jax.experimental import pallas as pl
from jax.experimental.pallas import tpu as pltpu
from jax.sharding import PartitionSpec as P

NSUB = 2
LEV = 58
HALF = 64
SLOTS = 32
N_GRP = 64
N_MEM = 12
ROWS = 4
POINTS = 32
COLS = SLOTS * N_MEM
HIGH = lax.Precision.HIGHEST
VMEM = pl.BlockSpec(memory_space=pltpu.VMEM)
SMEM = pl.BlockSpec(memory_space=pltpu.SMEM)
F32 = jnp.float32


def derivative_table():
    nodes = np.array([-1.0, -1.0 / np.sqrt(5.0), 1.0 / np.sqrt(5.0), 1.0])
    table = np.zeros((4, 4))
    for i in range(4):
        for j in range(4):
            if i == j:
                table[i, j] = sum(1.0 / (nodes[j] - nodes[k]) for k in range(4) if k != j)
            else:
                top = np.prod([nodes[i] - nodes[k] for k in range(4) if k not in (i, j)])
                low = np.prod([nodes[j] - nodes[k] for k in range(4) if k != j])
                table[i, j] = top / low
    return table.astype(np.float32)


def iota(shape, dim):
    return lax.broadcasted_iota(jnp.int32, shape, dim)


def dot(a, b):
    return jnp.dot(a, b, precision=HIGH, preferred_element_type=F32)


def dot_t(a, b):
    return lax.dot_general(a, b, (((0,), (0,)), ((), ())), precision=HIGH, preferred_element_type=F32)


def to_column(row):
    n = row.shape[1]
    return jnp.sum(jnp.where(iota((n, n), 0) == iota((n, n), 1), row, 0.0), axis=1, keepdims=True)


def both_kinds(heat, moist):
    gap = jnp.zeros((heat.shape[0], HALF - LEV), F32)
    return jnp.concatenate([heat, gap, moist, gap], axis=1)


def bucket_kernel(migrate, state, out):
    for s in range(SLOTS):
        group = lax.div(migrate[s], COLS)
        out[pl.ds(group * LEV, LEV), :] = state[pl.ds(s, LEV, stride=SLOTS), :]


def weigh_kernel(dyn, wind, mass, table, out):
    field = both_kinds(dyn[0].reshape(ROWS * POINTS, LEV), dyn[1].reshape(ROWS * POINTS, LEV))
    blow = wind[...].reshape(ROWS * POINTS, LEV)
    slope = dot(table[...], field)
    column = jnp.concatenate([to_column(mass[y : y + 1, :]) for y in range(ROWS)], axis=0)
    weighed = column * (-both_kinds(blow, blow) * slope)
    lane = iota((ROWS * POINTS, 2 * HALF), 1)
    out[...] = jnp.where(lane == LEV, column, weighed).reshape(ROWS, POINTS, 2 * HALF)


def assemble_kernel(own, before, after, batch, inner, payload):
    rows = [own[0] + before[0], own[1], own[2], own[3] + after[0]]
    point = iota((POINTS, 2 * HALF), 0)
    means, edges = [], []
    for y, row in enumerate(rows):
        opening = (point % 4 == 0) & (point > 0)
        closing = (point % 4 == 3) & (point < POINTS - 1)
        full = (
            row
            + jnp.where(opening, pltpu.roll(row, 1, 0), 0.0)
            + jnp.where(closing, pltpu.roll(row, POINTS - 1, 0), 0.0)
        )
        ratio = full / full[:, LEV : LEV + 1]
        inner[y] = ratio
        means.append(jnp.where((point == 0) | (point == POINTS - 1), 0.0, ratio))
        edges.append(row)
    col, pt = iota((SLOTS, ROWS * POINTS), 0), iota((SLOTS, ROWS * POINTS), 1)
    inside = (col // 16 == pt // (2 * POINTS)) & (col % 16 == (pt % POINTS) // 2)
    average = jnp.where(inside, 0.25, 0.0).astype(F32)
    forcing = dot(average, jnp.concatenate(means, axis=0))
    left = [row[0:1] for row in edges]
    right = [row[POINTS - 1 : POINTS] for row in edges]
    lane = iota((SLOTS, 2 * HALF), 1)
    forcing = jnp.where(lane == LEV, to_column(batch[...].astype(F32)), forcing)
    payload[...] = jnp.concatenate([forcing] + left + right, axis=0)


def forcing_kernel(gathered, batch, migrate, steps, force, edge, send):
    rows = []
    for d in range(N_MEM):
        right = gathered[d, SLOTS + ROWS : SLOTS + 2 * ROWS, :]
        left = gathered[(d + 1) % N_MEM, SLOTS : SLOTS + ROWS, :]
        both = right + left
        rows.append(both / both[:, LEV : LEV + 1])
    joined = jnp.concatenate(rows, axis=0)
    edge[...] = joined
    columns = gathered[:, :SLOTS, :].reshape(COLS, 2 * HALF)
    slot = batch[...]
    pick = jnp.where(iota((COLS, SLOTS), 0) == slot, 1.0, 0.0).astype(F32)
    e = iota((N_MEM * ROWS, SLOTS), 0)
    dev, half = e // ROWS, (e % ROWS) // 2
    ahead = jnp.where(dev == N_MEM - 1, 0, dev + 1)
    last = slot == dev * SLOTS + half * 16 + 15
    first = slot == ahead * SLOTS + half * 16
    pick_edge = jnp.where(last, 0.25, 0.0) + jnp.where(first, 0.25, 0.0)
    forced = dot_t(pick, columns) + dot_t(pick_edge, joined)
    new = migrate[...]
    place = to_column((new & (SLOTS - 1)).astype(F32)) + 1.0
    count = to_column(steps[...].astype(F32))
    lane = iota((SLOTS, 2 * HALF), 1)
    forced = jnp.where(lane == LEV, place, jnp.where(lane == LEV + 1, count, forced))
    force[...] = forced
    group = jnp.floor((new.astype(F32) + 0.5) * (1.0 / COLS)).astype(jnp.int32)
    goes = jnp.where(iota((N_GRP, SLOTS), 0) == group, 1.0, 0.0).astype(F32)
    send[...] = dot(goes, forced)


def neighbours_table():
    lanes = 2 * HALF
    table = np.zeros((lanes, 2 * lanes))
    for base in (0, HALF):
        for c in range(HALF):
            table[base + (c + 1) % HALF, base + c] += 1.0
            table[base + (c - 1) % HALF, base + c] += 1.0
            table[c, lanes + base + c] -= 1.0
            table[HALF + c, lanes + base + c] += 1.0
    return np.concatenate([table, table], axis=0).astype(jnp.bfloat16)


def means_table():
    same = np.kron(np.eye(2), np.ones((HALF, HALF))) / HALF
    return np.concatenate([same, same], axis=0).astype(jnp.bfloat16)


def two_parts(value):
    lead = value.astype(jnp.bfloat16)
    trail = (value - lead.astype(F32)).astype(jnp.bfloat16)
    return jnp.concatenate([lead, trail], axis=1)


CHUNKS = [(0, 8), (8, 8), (16, 8), (24, 8), (32, 8), (40, 8), (48, 8), (56, 2)]


def substep(source, first, count, forced, active, table):
    rows = count * SLOTS
    at = lambda l, n: source[l * SLOTS : (l + n) * SLOTS, :]
    current = at(first, count)
    if first + count < LEV:
        upper = at(first + 1, count)
    else:
        upper = jnp.concatenate([at(first + 1, count - 1), at(LEV - 1, 1)], axis=0)
    if first > 0:
        lower = at(first - 1, count)
    else:
        lower = jnp.concatenate([at(0, 1), at(0, count - 1)], axis=0)
    mixed = jnp.dot(two_parts(current), table, preferred_element_type=F32)
    side, gap = mixed[:, : 2 * HALF], mixed[:, 2 * HALF :]
    soft = jnp.maximum(gap, 0.0) + jnp.log(1.0 + jnp.exp(-jnp.abs(gap)))
    sign = jnp.where(iota((rows, 2 * HALF), 1) < HALF, 0.05, -0.1)
    updated = 0.5 * current + forced + 0.15 * side + 0.1 * (upper + lower) + sign * soft
    on = jnp.broadcast_to(active, (SLOTS, 2 * HALF))
    return jnp.where(jnp.concatenate([on] * count, axis=0), updated, current)


def spread(quarter, first, count):
    lane = iota((SLOTS, 2 * HALF), 1)
    return jnp.concatenate(
        [
            jnp.take_along_axis(quarter, (lane & HALF) + level, axis=1, mode="promise_in_bounds")
            for level in range(first, first + count)
        ],
        axis=0,
    )


def run_cloud(state, force, table, middle, keep):
    steps = force[:, LEV + 1 : LEV + 2]
    quarter = 0.25 * force[...]
    for first, count in CHUNKS:
        forced = spread(quarter, first, count)
        rows = pl.ds(first * SLOTS, count * SLOTS)
        middle[rows, :] = substep(state, first, count, forced, steps > 0.5, table[...])
    for first, count in CHUNKS:
        forced = spread(quarter, first, count)
        keep(first, count, substep(middle, first, count, forced, steps > 1.5, table[...]))


def tendency_kernel(state, force, table, means, send, middle):
    column = iota((SLOTS, 2 * HALF), 1) & (HALF - 1)
    send[...] = jnp.zeros((SLOTS, 2 * HALF), F32)

    def keep(first, count, stepped):
        change = stepped - state[first * SLOTS : (first + count) * SLOTS, :]
        mean = jnp.dot(two_parts(change), means[...], preferred_element_type=F32)
        total = send[...]
        for i in range(count):
            total = jnp.where(column == first + i, mean[i * SLOTS : (i + 1) * SLOTS, :], total)
        send[...] = total

    run_cloud(state, force, table, middle, keep)


def select_kernel(rest, force, origin):
    slot = (iota((N_GRP, SLOTS), 1) + 1).astype(F32)
    pick = jnp.where(rest[:, LEV : LEV + 1] == slot, 1.0, 0.0).astype(F32)
    force[...] = dot_t(pick, rest[...])
    group = iota((N_GRP, SLOTS), 0).astype(F32)
    origin[...] = jnp.sum(pick * group, axis=0, keepdims=True).astype(jnp.int32)


def arrive_kernel(source, main, force, table, out, held, middle):
    for j in range(SLOTS):
        held[pl.ds(j, LEV, stride=SLOTS), :] = main[pl.ds(source[0, j] * LEV, LEV), :]

    def keep(first, count, stepped):
        out[first * SLOTS : (first + count) * SLOTS, :] = stepped

    run_cloud(held, force, table, middle, keep)


def next_kernel(dyn, inner, edge, out):
    me = lax.axis_index("mem")
    behind = lax.rem(me + N_MEM - 1, N_MEM)
    for y in range(ROWS):
        point = iota((POINTS, 2 * HALF), 0)
        left = edge[pl.ds(behind * ROWS + y, 1), :]
        right = edge[pl.ds(me * ROWS + y, 1), :]
        ratio = jnp.where(point == 0, left, jnp.where(point == POINTS - 1, right, inner[y]))
        out[0, y] = dyn[0, y] + 0.2 * ratio[:, :LEV]
        out[1, y] = dyn[1, y] + 0.2 * ratio[:, HALF : HALF + LEV]


def column_kernel(tendency, gathered, out):
    serves = gathered[:, :SLOTS, :].reshape(COLS, 2 * HALF)[:, LEV : LEV + 1]
    column = (iota((COLS, SLOTS), 1) + lax.axis_index("mem") * SLOTS).astype(F32)
    pick = jnp.where(serves == column, 1.0, 0.0).astype(F32)
    mine = dot_t(pick, tendency[...])
    out[0] = mine[:, :LEV]
    out[1] = mine[:, HALF : HALF + LEV]


def call(kernel, shapes, specs, scratch=()):
    many = isinstance(shapes, list)
    out = [jax.ShapeDtypeStruct(s, F32) for s in shapes] if many else jax.ShapeDtypeStruct(shapes, F32)
    return pl.pallas_call(
        kernel,
        out_shape=out,
        in_specs=specs,
        out_specs=[VMEM] * len(shapes) if many else VMEM,
        scratch_shapes=[pltpu.VMEM(s, F32) for s in scratch],
        compiler_params=pltpu.CompilerParams(vmem_limit_bytes=24 * 2**20),
    )


def on_device(dyn_state, wind_speed, mass_weight, crm_state, batch_map, sub_steps, migrate_to):
    lanes = 2 * HALF
    dyn = dyn_state.transpose(0, 2, 3, 1)
    wind = wind_speed.transpose(1, 2, 0)
    state = crm_state.transpose(1, 0, 2).reshape(LEV * SLOTS, lanes)
    batch, steps, moves = (a.reshape(1, SLOTS) for a in (batch_map, sub_steps, migrate_to))
    table = jnp.asarray(np.kron(np.eye(ROWS * POINTS // 4), derivative_table()).astype(np.float32))

    weighed = call(weigh_kernel, (ROWS, POINTS, lanes), [VMEM] * 4)(dyn, wind, mass_weight, table)
    weighed, state_later = lax.optimization_barrier((weighed, state))
    buckets = call(bucket_kernel, (N_GRP * LEV, lanes), [SMEM, VMEM])(migrate_to, state_later)
    up = [(i, (i + 1) % N_GRP) for i in range(N_GRP)]
    down = [(j, i) for i, j in up]
    before = lax.ppermute(weighed[ROWS - 1 :], "grp", up)
    after = lax.ppermute(weighed[:1], "grp", down)
    buckets, before, after = lax.optimization_barrier((buckets, before, after))
    main = lax.all_to_all(buckets.reshape(N_GRP, LEV // 2, 2, lanes), "grp", 0, 0, tiled=True)
    inner, payload = call(
        assemble_kernel, [(ROWS, POINTS, lanes), (SLOTS + 2 * ROWS, lanes)], [VMEM] * 4
    )(weighed, before, after, batch)
    gathered = lax.all_gather(payload, "mem", axis=0)
    force, edge, send = call(
        forcing_kernel, [(SLOTS, lanes), (N_MEM * ROWS, lanes), (N_GRP, lanes)], [VMEM] * 4
    )(gathered, batch, moves, steps)
    cells = LEV * SLOTS
    mix, means = jnp.asarray(neighbours_table()), jnp.asarray(means_table())
    tendency = call(tendency_kernel, (SLOTS, lanes), [VMEM] * 4, [(cells, lanes)])(state, force, mix, means)
    tendencies = lax.all_gather(tendency, "mem", axis=0, tiled=True)
    send, main, tendencies = lax.optimization_barrier((send, main, tendencies))
    rest = lax.all_to_all(send.reshape(N_GRP, 1, lanes), "grp", 0, 0, tiled=True)
    dyn_next = call(next_kernel, (2, ROWS, POINTS, LEV), [VMEM] * 3)(dyn, inner, edge)
    phys = call(column_kernel, (2, SLOTS, LEV), [VMEM] * 2)(tendencies, gathered)

    brought, origin = pl.pallas_call(
        select_kernel,
        out_shape=[jax.ShapeDtypeStruct((SLOTS, lanes), F32), jax.ShapeDtypeStruct((1, SLOTS), jnp.int32)],
        in_specs=[VMEM],
        out_specs=[VMEM] * 2,
        compiler_params=pltpu.CompilerParams(vmem_limit_bytes=24 * 2**20),
    )(rest.reshape(N_GRP, lanes))
    new = call(arrive_kernel, (cells, lanes), [SMEM, VMEM, VMEM, VMEM], [(cells, lanes)] * 2)(
        origin, main.reshape(N_GRP * LEV, lanes), brought, mix
    )
    crm_next = new.reshape(LEV, SLOTS, lanes).transpose(1, 0, 2)
    return (dyn_next.transpose(0, 3, 1, 2), phys.transpose(0, 2, 1), crm_next)


def solution(mesh):
    placed = (
        P(None, None, "grp", "mem"),
        P(None, "grp", "mem"),
        P("grp", "mem"),
        P(("grp", "mem"), None, None),
        P(("grp", "mem")),
        P(("grp", "mem")),
        P(("grp", "mem")),
    )
    return jax.shard_map(
        on_device,
        mesh=mesh,
        in_specs=placed,
        out_specs=(
            P(None, None, "grp", "mem"),
            P(None, None, ("grp", "mem")),
            P(("grp", "mem"), None, None),
        ),
        check_vma=False,
    )
```

```python
import jax
import jax.numpy as jnp
import numpy as np
from jax import lax
from jax.experimental import pallas as pl
from jax.experimental.pallas import tpu as pltpu
from jax.sharding import PartitionSpec as P

NSUB = 2
LEV = 58
HALF = 64
SLOTS = 32
N_GRP = 64
N_MEM = 12
ROWS = 4
POINTS = 32
COLS = SLOTS * N_MEM
HIGH = lax.Precision.HIGHEST
VMEM = pl.BlockSpec(memory_space=pltpu.VMEM)
SMEM = pl.BlockSpec(memory_space=pltpu.SMEM)
HBM = pl.BlockSpec(memory_space=pltpu.HBM)
F32 = jnp.float32


def derivative_table():
    nodes = np.array([-1.0, -1.0 / np.sqrt(5.0), 1.0 / np.sqrt(5.0), 1.0])
    table = np.zeros((4, 4))
    for i in range(4):
        for j in range(4):
            if i == j:
                table[i, j] = sum(1.0 / (nodes[j] - nodes[k]) for k in range(4) if k != j)
            else:
                top = np.prod([nodes[i] - nodes[k] for k in range(4) if k not in (i, j)])
                low = np.prod([nodes[j] - nodes[k] for k in range(4) if k != j])
                table[i, j] = top / low
    return table.astype(np.float32)


def iota(shape, dim):
    return lax.broadcasted_iota(jnp.int32, shape, dim)


def dot(a, b):
    return jnp.dot(a, b, precision=HIGH, preferred_element_type=F32)


def dot_t(a, b):
    return lax.dot_general(a, b, (((0,), (0,)), ((), ())), precision=HIGH, preferred_element_type=F32)


def to_column(row):
    n = row.shape[1]
    return jnp.sum(jnp.where(iota((n, n), 0) == iota((n, n), 1), row, 0.0), axis=1, keepdims=True)


def both_kinds(heat, moist):
    gap = jnp.zeros((heat.shape[0], HALF - LEV), F32)
    return jnp.concatenate([heat, gap, moist, gap], axis=1)


def bucket_kernel(migrate, state, out, done):
    copies = []
    for s in range(SLOTS):
        group = lax.div(migrate[s], COLS)
        copies.append(
            pltpu.make_async_copy(state.at[:, s], out.at[group, pl.ds(0, LEV)], done.at[s])
        )
        copies[-1].start()
    for copy in copies:
        copy.wait()


def weigh_kernel(dyn_at, wind_at, mass_at, table_at, batch_at, out, top, end, dyn, wind, mass, table, batch, done):
    pairs = [(dyn_at, dyn), (wind_at, wind), (mass_at, mass), (table_at, table), (batch_at, batch)]
    copies = [pltpu.make_async_copy(a, b, done.at[i]) for i, (a, b) in enumerate(pairs)]
    for copy in copies:
        copy.start()
    for copy in copies:
        copy.wait()
    field = both_kinds(dyn[0].reshape(ROWS * POINTS, LEV), dyn[1].reshape(ROWS * POINTS, LEV))
    blow = wind[...].reshape(ROWS * POINTS, LEV)
    slope = dot(table[...], field)
    column = jnp.concatenate([to_column(mass[y : y + 1, :]) for y in range(ROWS)], axis=0)
    weighed = column * (-both_kinds(blow, blow) * slope)
    lane = iota((ROWS * POINTS, 2 * HALF), 1)
    serves = jnp.concatenate([to_column(batch[...].astype(F32))] * ROWS, axis=0)
    spare = jnp.where(lane == LEV, column, serves)
    weighed = jnp.where((lane == LEV) | (lane == LEV + 1), spare, weighed)
    weighed = weighed.reshape(ROWS, POINTS, 2 * HALF)
    out[...] = weighed
    top[0] = weighed[0]
    end[0] = weighed[ROWS - 1]


def assemble_kernel(own, before, after, inner, payload):
    rows = [own[0] + before[0], own[1], own[2], own[3] + after[0]]
    point = iota((POINTS, 2 * HALF), 0)
    means, edges = [], []
    for y, row in enumerate(rows):
        opening = (point % 4 == 0) & (point > 0)
        closing = (point % 4 == 3) & (point < POINTS - 1)
        full = (
            row
            + jnp.where(opening, pltpu.roll(row, 1, 0), 0.0)
            + jnp.where(closing, pltpu.roll(row, POINTS - 1, 0), 0.0)
        )
        ratio = full / full[:, LEV : LEV + 1]
        inner[y] = ratio
        means.append(jnp.where((point == 0) | (point == POINTS - 1), 0.0, ratio))
        edges.append(row)
    col, pt = iota((SLOTS, ROWS * POINTS), 0), iota((SLOTS, ROWS * POINTS), 1)
    inside = (col // 16 == pt // (2 * POINTS)) & (col % 16 == (pt % POINTS) // 2)
    average = jnp.where(inside, 0.25, 0.0).astype(F32)
    forcing = dot(average, jnp.concatenate(means, axis=0))
    left = [row[0:1] for row in edges]
    right = [row[POINTS - 1 : POINTS] for row in edges]
    lane = iota((SLOTS, 2 * HALF), 1)
    forcing = jnp.where(lane == LEV, own[0][:, LEV + 1 : LEV + 2], forcing)
    whole = jnp.concatenate([forcing] + left + right, axis=0)
    for d in range(N_MEM):
        payload[d] = whole


def forcing_kernel(gathered, batch, migrate, steps, buckets, force, edge, filled, row, done):
    rows = []
    for d in range(N_MEM):
        right = gathered[d, SLOTS + ROWS : SLOTS + 2 * ROWS, :]
        left = gathered[(d + 1) % N_MEM, SLOTS : SLOTS + ROWS, :]
        both = right + left
        rows.append(both / both[:, LEV : LEV + 1])
    joined = jnp.concatenate(rows, axis=0)
    edge[...] = joined
    columns = gathered[:, :SLOTS, :].reshape(COLS, 2 * HALF)
    slot = batch[...]
    pick = jnp.where(iota((COLS, SLOTS), 0) == slot, 1.0, 0.0).astype(F32)
    e = iota((N_MEM * ROWS, SLOTS), 0)
    dev, half = e // ROWS, (e % ROWS) // 2
    ahead = jnp.where(dev == N_MEM - 1, 0, dev + 1)
    last = slot == dev * SLOTS + half * 16 + 15
    first = slot == ahead * SLOTS + half * 16
    pick_edge = jnp.where(last, 0.25, 0.0) + jnp.where(first, 0.25, 0.0)
    forced = dot_t(pick, columns) + dot_t(pick_edge, joined)
    new = migrate[...]
    place = to_column((new & (SLOTS - 1)).astype(F32)) + 1.0
    count = to_column(steps[...].astype(F32))
    lane = iota((SLOTS, 2 * HALF), 1)
    forced = jnp.where(lane == LEV, place, jnp.where(lane == LEV + 1, count, forced))
    force[...] = forced
    group = jnp.floor((new.astype(F32) + 0.5) * (1.0 / COLS)).astype(jnp.int32)
    goes = jnp.where(iota((N_GRP, SLOTS), 0) == group, 1.0, 0.0).astype(F32)
    row[...] = dot(goes, forced).reshape(N_GRP, 1, 2 * HALF)
    copy = pltpu.make_async_copy(row, filled.at[:, LEV], done)
    copy.start()
    copy.wait()


def neighbours_table():
    lanes = 2 * HALF
    table = np.zeros((lanes, 2 * lanes))
    for base in (0, HALF):
        for c in range(HALF):
            table[base + (c + 1) % HALF, base + c] += 1.0
            table[base + (c - 1) % HALF, base + c] += 1.0
            table[c, lanes + base + c] -= 1.0
            table[HALF + c, lanes + base + c] += 1.0
    return np.concatenate([table, table], axis=0).astype(jnp.bfloat16)


def means_table():
    same = np.kron(np.eye(2), np.ones((HALF, HALF))) / HALF
    return np.concatenate([same, same], axis=0).astype(jnp.bfloat16)


def two_parts(value):
    lead = value.astype(jnp.bfloat16)
    trail = (value - lead.astype(F32)).astype(jnp.bfloat16)
    return jnp.concatenate([lead, trail], axis=1)


SENT = LEV + 1
CHUNKS = [(0, 8), (8, 8), (16, 8), (24, 8), (32, 8), (40, 8), (48, 8), (56, 2)]


def substep(source, first, count, forced, active, table):
    rows = count * SLOTS
    at = lambda l, n: source[l * SLOTS : (l + n) * SLOTS, :]
    current = at(first, count)
    if first + count < LEV:
        upper = at(first + 1, count)
    else:
        upper = jnp.concatenate([at(first + 1, count - 1), at(LEV - 1, 1)], axis=0)
    if first > 0:
        lower = at(first - 1, count)
    else:
        lower = jnp.concatenate([at(0, 1), at(0, count - 1)], axis=0)
    mixed = jnp.dot(two_parts(current), table, preferred_element_type=F32)
    side, gap = mixed[:, : 2 * HALF], mixed[:, 2 * HALF :]
    soft = jnp.maximum(gap, 0.0) + jnp.log(1.0 + jnp.exp(-jnp.abs(gap)))
    sign = jnp.where(iota((rows, 2 * HALF), 1) < HALF, 0.05, -0.1)
    updated = 0.5 * current + forced + 0.15 * side + 0.1 * (upper + lower) + sign * soft
    on = jnp.broadcast_to(active, (SLOTS, 2 * HALF))
    return jnp.where(jnp.concatenate([on] * count, axis=0), updated, current)


def spread(quarter, first, count):
    lane = iota((SLOTS, 2 * HALF), 1)
    return jnp.concatenate(
        [
            jnp.take_along_axis(quarter, (lane & HALF) + level, axis=1, mode="promise_in_bounds")
            for level in range(first, first + count)
        ],
        axis=0,
    )


def run_cloud(state, force, table, middle, keep):
    steps = force[:, LEV + 1 : LEV + 2]
    quarter = 0.25 * force[...]
    for first, count in CHUNKS:
        forced = spread(quarter, first, count)
        rows = pl.ds(first * SLOTS, count * SLOTS)
        middle[rows, :] = substep(state, first, count, forced, steps > 0.5, table[...])
    for first, count in CHUNKS:
        forced = spread(quarter, first, count)
        keep(first, count, substep(middle, first, count, forced, steps > 1.5, table[...]))


def tendency_kernel(state, force, table, means, send, middle):
    column = iota((SLOTS, 2 * HALF), 1) & (HALF - 1)
    send[...] = jnp.zeros((SLOTS, 2 * HALF), F32)

    def keep(first, count, stepped):
        change = stepped - state[first * SLOTS : (first + count) * SLOTS, :]
        mean = jnp.dot(two_parts(change), means[...], preferred_element_type=F32)
        total = send[...]
        for i in range(count):
            total = jnp.where(column == first + i, mean[i * SLOTS : (i + 1) * SLOTS, :], total)
        send[...] = total

    run_cloud(state, force, table, middle, keep)


def arrive_kernel(main, table, out, held, middle, force, row, origin, done):
    last = main[pl.ds(LEV, N_GRP, stride=SENT), :]
    slot = (iota((N_GRP, SLOTS), 1) + 1).astype(F32)
    pick = jnp.where(last[:, LEV : LEV + 1] == slot, 1.0, 0.0).astype(F32)
    group = iota((N_GRP, SLOTS), 0).astype(F32)
    row[...] = jnp.sum(pick * group, axis=0, keepdims=True).astype(jnp.int32)
    copy = pltpu.make_async_copy(row, origin, done)
    copy.start()
    force[...] = dot_t(pick, last)
    copy.wait()
    for j in range(SLOTS):
        held[pl.ds(j, LEV, stride=SLOTS), :] = main[pl.ds(origin[0, j] * SENT, LEV), :]

    def keep(first, count, stepped):
        out[first * SLOTS : (first + count) * SLOTS, :] = stepped

    run_cloud(held, force, table, middle, keep)


def next_kernel(dyn, inner, edge, out):
    me = lax.axis_index("mem")
    behind = lax.rem(me + N_MEM - 1, N_MEM)
    for y in range(ROWS):
        point = iota((POINTS, 2 * HALF), 0)
        left = edge[pl.ds(behind * ROWS + y, 1), :]
        right = edge[pl.ds(me * ROWS + y, 1), :]
        ratio = jnp.where(point == 0, left, jnp.where(point == POINTS - 1, right, inner[y]))
        out[0, y] = dyn[0, y] + 0.2 * ratio[:, :LEV]
        out[1, y] = dyn[1, y] + 0.2 * ratio[:, HALF : HALF + LEV]


def column_kernel(tendency, gathered, out):
    serves = gathered[:, :SLOTS, :].reshape(COLS, 2 * HALF)[:, LEV : LEV + 1]
    column = (iota((COLS, SLOTS), 1) + lax.axis_index("mem") * SLOTS).astype(F32)
    pick = jnp.where(serves == column, 1.0, 0.0).astype(F32)
    mine = dot_t(pick, tendency[...])
    out[0] = mine[:, :LEV]
    out[1] = mine[:, HALF : HALF + LEV]


def call(kernel, shapes, specs, scratch=(), out_specs=None, aliases=None, limit=24):
    many = isinstance(shapes, list)
    out = [jax.ShapeDtypeStruct(s, F32) for s in shapes] if many else jax.ShapeDtypeStruct(shapes, F32)
    return pl.pallas_call(
        kernel,
        out_shape=out,
        in_specs=specs,
        out_specs=out_specs or ([VMEM] * len(shapes) if many else VMEM),
        scratch_shapes=[pltpu.VMEM(s, F32) if isinstance(s, tuple) else s for s in scratch],
        input_output_aliases=aliases or {},
        compiler_params=pltpu.CompilerParams(vmem_limit_bytes=limit * 2**20),
    )


def on_device(dyn_state, wind_speed, mass_weight, crm_state, batch_map, sub_steps, migrate_to):
    lanes = 2 * HALF
    dyn = dyn_state.transpose(0, 2, 3, 1)
    wind = wind_speed.transpose(1, 2, 0)
    state = crm_state.transpose(1, 0, 2).reshape(LEV * SLOTS, lanes)
    batch, steps, moves = (a.reshape(1, SLOTS) for a in (batch_map, sub_steps, migrate_to))
    table = jnp.asarray(np.kron(np.eye(ROWS * POINTS // 4), derivative_table()).astype(np.float32))

    cells = LEV * SLOTS
    dma = pltpu.SemaphoreType.DMA
    ints = pltpu.VMEM((1, SLOTS), jnp.int32)
    weighed, top, end = call(
        weigh_kernel,
        [(ROWS, POINTS, lanes), (1, POINTS, lanes), (1, POINTS, lanes)],
        [HBM] * 5,
        [(2, ROWS, POINTS, LEV), (ROWS, POINTS, LEV), (ROWS, POINTS), table.shape, ints, dma((5,))],
        limit=60,
    )(dyn, wind, mass_weight, table, batch)
    weighed, state_later = lax.optimization_barrier((weighed, state))
    buckets = call(bucket_kernel, (N_GRP, SENT, 1, lanes), [SMEM, HBM], [dma((SLOTS,))], HBM, limit=60)(
        migrate_to, state_later.reshape(LEV, SLOTS, 1, lanes)
    )
    up = [(i, (i + 1) % N_GRP) for i in range(N_GRP)]
    down = [(j, i) for i, j in up]
    before = lax.ppermute(end, "grp", up)
    after = lax.ppermute(top, "grp", down)
    inner, payload = call(
        assemble_kernel, [(ROWS, POINTS, lanes), (N_MEM, SLOTS + 2 * ROWS, lanes)], [VMEM] * 3
    )(weighed, before, after)
    gathered = lax.all_to_all(payload, "mem", 0, 0, tiled=True)
    force, edge, filled = call(
        forcing_kernel,
        [(SLOTS, lanes), (N_MEM * ROWS, lanes), (N_GRP, SENT, 1, lanes)],
        [VMEM] * 4 + [HBM],
        [(N_GRP, 1, lanes), dma],
        [VMEM, VMEM, HBM],
        {4: 2},
        limit=61,
    )(gathered, batch, moves, steps, buckets)
    main = lax.all_to_all(filled, "grp", 0, 0, tiled=True)
    mix, means = jnp.asarray(neighbours_table()), jnp.asarray(means_table())
    tendency = call(tendency_kernel, (SLOTS, lanes), [VMEM] * 4, [(cells, lanes)])(state, force, mix, means)
    tendencies = lax.all_gather(tendency, "mem", axis=0, tiled=True)
    dyn_next = call(next_kernel, (2, ROWS, POINTS, LEV), [VMEM] * 3)(dyn, inner, edge)
    phys = call(column_kernel, (2, SLOTS, LEV), [VMEM] * 2)(tendencies, gathered)
    new = call(
        arrive_kernel,
        (cells, lanes),
        [VMEM] * 2,
        [(cells, lanes)] * 2
        + [(SLOTS, lanes), ints, pltpu.SMEM((1, SLOTS), jnp.int32), dma],
    )(main.reshape(N_GRP * SENT, lanes), mix)
    crm_next = new.reshape(LEV, SLOTS, lanes).transpose(1, 0, 2)
    return (dyn_next.transpose(0, 3, 1, 2), phys.transpose(0, 2, 1), crm_next)


def solution(mesh):
    placed = (
        P(None, None, "grp", "mem"),
        P(None, "grp", "mem"),
        P("grp", "mem"),
        P(("grp", "mem"), None, None),
        P(("grp", "mem")),
        P(("grp", "mem")),
        P(("grp", "mem")),
    )
    return jax.shard_map(
        on_device,
        mesh=mesh,
        in_specs=placed,
        out_specs=(
            P(None, None, "grp", "mem"),
            P(None, None, ("grp", "mem")),
            P(("grp", "mem"), None, None),
        ),
        check_vma=False,
    )
```

```python
import jax
import jax.numpy as jnp
import numpy as np
from jax import lax
from jax.experimental import pallas as pl
from jax.experimental.pallas import tpu as pltpu
from jax.sharding import PartitionSpec as P

NSUB = 2
LEV = 58
HALF = 64
SLOTS = 32
N_GRP = 64
N_MEM = 12
ROWS = 4
POINTS = 32
COLS = SLOTS * N_MEM
HIGH = lax.Precision.HIGHEST
VMEM = pl.BlockSpec(memory_space=pltpu.VMEM)
SMEM = pl.BlockSpec(memory_space=pltpu.SMEM)
HBM = pl.BlockSpec(memory_space=pltpu.HBM)
F32 = jnp.float32


def derivative_table():
    nodes = np.array([-1.0, -1.0 / np.sqrt(5.0), 1.0 / np.sqrt(5.0), 1.0])
    table = np.zeros((4, 4))
    for i in range(4):
        for j in range(4):
            if i == j:
                table[i, j] = sum(1.0 / (nodes[j] - nodes[k]) for k in range(4) if k != j)
            else:
                top = np.prod([nodes[i] - nodes[k] for k in range(4) if k not in (i, j)])
                low = np.prod([nodes[j] - nodes[k] for k in range(4) if k != j])
                table[i, j] = top / low
    return table.astype(np.float32)


def iota(shape, dim):
    return lax.broadcasted_iota(jnp.int32, shape, dim)


def dot(a, b):
    return jnp.dot(a, b, precision=HIGH, preferred_element_type=F32)


def dot_t(a, b):
    return lax.dot_general(a, b, (((0,), (0,)), ((), ())), precision=HIGH, preferred_element_type=F32)


def to_column(row):
    n = row.shape[1]
    return jnp.sum(jnp.where(iota((n, n), 0) == iota((n, n), 1), row, 0.0), axis=1, keepdims=True)


def both_kinds(heat, moist):
    gap = jnp.zeros((heat.shape[0], HALF - LEV), F32)
    return jnp.concatenate([heat, gap, moist, gap], axis=1)


def bucket_kernel(migrate, state, out):
    for s in range(SLOTS):
        group = lax.div(migrate[s], COLS)
        out[pl.ds(group * SENT, LEV), :] = state[pl.ds(s, LEV, stride=SLOTS), :]


def weigh_kernel(dyn_at, wind_at, mass_at, table_at, batch_at, out, top, end, dyn, wind, mass, table, batch, done):
    pairs = [(dyn_at, dyn), (wind_at, wind), (mass_at, mass), (table_at, table), (batch_at, batch)]
    copies = [pltpu.make_async_copy(a, b, done.at[i]) for i, (a, b) in enumerate(pairs)]
    for copy in copies:
        copy.start()
    for copy in copies:
        copy.wait()
    field = both_kinds(dyn[0].reshape(ROWS * POINTS, LEV), dyn[1].reshape(ROWS * POINTS, LEV))
    blow = wind[...].reshape(ROWS * POINTS, LEV)
    slope = dot(table[...], field)
    column = jnp.concatenate([to_column(mass[y : y + 1, :]) for y in range(ROWS)], axis=0)
    weighed = column * (-both_kinds(blow, blow) * slope)
    lane = iota((ROWS * POINTS, 2 * HALF), 1)
    serves = jnp.concatenate([to_column(batch[...].astype(F32))] * ROWS, axis=0)
    spare = jnp.where(lane == LEV, column, serves)
    weighed = jnp.where((lane == LEV) | (lane == LEV + 1), spare, weighed)
    weighed = weighed.reshape(ROWS, POINTS, 2 * HALF)
    out[...] = weighed
    top[0] = weighed[0]
    end[0] = weighed[ROWS - 1]


def assemble_kernel(own, before, after, inner, payload):
    rows = [own[0] + before[0], own[1], own[2], own[3] + after[0]]
    point = iota((POINTS, 2 * HALF), 0)
    means, edges = [], []
    for y, row in enumerate(rows):
        opening = (point % 4 == 0) & (point > 0)
        closing = (point % 4 == 3) & (point < POINTS - 1)
        full = (
            row
            + jnp.where(opening, pltpu.roll(row, 1, 0), 0.0)
            + jnp.where(closing, pltpu.roll(row, POINTS - 1, 0), 0.0)
        )
        ratio = full / full[:, LEV : LEV + 1]
        inner[y] = ratio
        means.append(jnp.where((point == 0) | (point == POINTS - 1), 0.0, ratio))
        edges.append(row)
    col, pt = iota((SLOTS, ROWS * POINTS), 0), iota((SLOTS, ROWS * POINTS), 1)
    inside = (col // 16 == pt // (2 * POINTS)) & (col % 16 == (pt % POINTS) // 2)
    average = jnp.where(inside, 0.25, 0.0).astype(F32)
    forcing = dot(average, jnp.concatenate(means, axis=0))
    left = [row[0:1] for row in edges]
    right = [row[POINTS - 1 : POINTS] for row in edges]
    lane = iota((SLOTS, 2 * HALF), 1)
    forcing = jnp.where(lane == LEV, own[0][:, LEV + 1 : LEV + 2], forcing)
    whole = jnp.concatenate([forcing] + left + right, axis=0)
    for d in range(N_MEM):
        payload[d] = whole


def forcing_kernel(gathered, batch, migrate, steps, buckets, force, edge, filled, row, done):
    rows = []
    for d in range(N_MEM):
        right = gathered[d, SLOTS + ROWS : SLOTS + 2 * ROWS, :]
        left = gathered[(d + 1) % N_MEM, SLOTS : SLOTS + ROWS, :]
        both = right + left
        rows.append(both / both[:, LEV : LEV + 1])
    joined = jnp.concatenate(rows, axis=0)
    edge[...] = joined
    columns = gathered[:, :SLOTS, :].reshape(COLS, 2 * HALF)
    slot = batch[...]
    pick = jnp.where(iota((COLS, SLOTS), 0) == slot, 1.0, 0.0).astype(F32)
    e = iota((N_MEM * ROWS, SLOTS), 0)
    dev, half = e // ROWS, (e % ROWS) // 2
    ahead = jnp.where(dev == N_MEM - 1, 0, dev + 1)
    last = slot == dev * SLOTS + half * 16 + 15
    first = slot == ahead * SLOTS + half * 16
    pick_edge = jnp.where(last, 0.25, 0.0) + jnp.where(first, 0.25, 0.0)
    forced = dot_t(pick, columns) + dot_t(pick_edge, joined)
    new = migrate[...]
    place = to_column((new & (SLOTS - 1)).astype(F32)) + 1.0
    count = to_column(steps[...].astype(F32))
    lane = iota((SLOTS, 2 * HALF), 1)
    forced = jnp.where(lane == LEV, place, jnp.where(lane == LEV + 1, count, forced))
    force[...] = forced
    group = jnp.floor((new.astype(F32) + 0.5) * (1.0 / COLS)).astype(jnp.int32)
    goes = jnp.where(iota((N_GRP, SLOTS), 0) == group, 1.0, 0.0).astype(F32)
    row[...] = dot(goes, forced).reshape(N_GRP, 1, 2 * HALF)
    copy = pltpu.make_async_copy(row, filled.at[:, LEV], done)
    copy.start()
    copy.wait()


def neighbours_table():
    lanes = 2 * HALF
    table = np.zeros((lanes, 2 * lanes))
    for base in (0, HALF):
        for c in range(HALF):
            table[base + (c + 1) % HALF, base + c] += 1.0
            table[base + (c - 1) % HALF, base + c] += 1.0
            table[c, lanes + base + c] -= 1.0
            table[HALF + c, lanes + base + c] += 1.0
    return np.concatenate([table, table], axis=0).astype(jnp.bfloat16)


def means_table():
    same = np.kron(np.eye(2), np.ones((HALF, HALF))) / HALF
    return np.concatenate([same, same], axis=0).astype(jnp.bfloat16)


def two_parts(value):
    lead = value.astype(jnp.bfloat16)
    trail = (value - lead.astype(F32)).astype(jnp.bfloat16)
    return jnp.concatenate([lead, trail], axis=1)


SENT = LEV + 1
CHUNKS = [(0, 8), (8, 8), (16, 8), (24, 8), (32, 8), (40, 8), (48, 8), (56, 2)]


def substep(source, first, count, forced, active, table):
    rows = count * SLOTS
    at = lambda l, n: source[l * SLOTS : (l + n) * SLOTS, :]
    current = at(first, count)
    if first + count < LEV:
        upper = at(first + 1, count)
    else:
        upper = jnp.concatenate([at(first + 1, count - 1), at(LEV - 1, 1)], axis=0)
    if first > 0:
        lower = at(first - 1, count)
    else:
        lower = jnp.concatenate([at(0, 1), at(0, count - 1)], axis=0)
    mixed = jnp.dot(two_parts(current), table, preferred_element_type=F32)
    side, gap = mixed[:, : 2 * HALF], mixed[:, 2 * HALF :]
    soft = jnp.maximum(gap, 0.0) + jnp.log(1.0 + jnp.exp(-jnp.abs(gap)))
    sign = jnp.where(iota((rows, 2 * HALF), 1) < HALF, 0.05, -0.1)
    updated = 0.5 * current + forced + 0.15 * side + 0.1 * (upper + lower) + sign * soft
    on = jnp.broadcast_to(active, (SLOTS, 2 * HALF))
    return jnp.where(jnp.concatenate([on] * count, axis=0), updated, current)


def spread(quarter, first, count):
    lane = iota((SLOTS, 2 * HALF), 1)
    return jnp.concatenate(
        [
            jnp.take_along_axis(quarter, (lane & HALF) + level, axis=1, mode="promise_in_bounds")
            for level in range(first, first + count)
        ],
        axis=0,
    )


def run_cloud(state, force, table, middle, keep):
    steps = force[:, LEV + 1 : LEV + 2]
    quarter = 0.25 * force[...]
    for first, count in CHUNKS:
        forced = spread(quarter, first, count)
        rows = pl.ds(first * SLOTS, count * SLOTS)
        middle[rows, :] = substep(state, first, count, forced, steps > 0.5, table[...])
    for first, count in CHUNKS:
        forced = spread(quarter, first, count)
        keep(first, count, substep(middle, first, count, forced, steps > 1.5, table[...]))


def tendency_kernel(state, force, table, means, send, middle):
    column = iota((SLOTS, 2 * HALF), 1) & (HALF - 1)
    send[...] = jnp.zeros((SLOTS, 2 * HALF), F32)

    def keep(first, count, stepped):
        change = stepped - state[first * SLOTS : (first + count) * SLOTS, :]
        mean = jnp.dot(two_parts(change), means[...], preferred_element_type=F32)
        total = send[...]
        for i in range(count):
            total = jnp.where(column == first + i, mean[i * SLOTS : (i + 1) * SLOTS, :], total)
        send[...] = total

    run_cloud(state, force, table, middle, keep)


def arrive_kernel(main, table, out, held, middle, force, row, origin, done):
    last = main[pl.ds(LEV, N_GRP, stride=SENT), :]
    slot = (iota((N_GRP, SLOTS), 1) + 1).astype(F32)
    pick = jnp.where(last[:, LEV : LEV + 1] == slot, 1.0, 0.0).astype(F32)
    group = iota((N_GRP, SLOTS), 0).astype(F32)
    row[...] = jnp.sum(pick * group, axis=0, keepdims=True).astype(jnp.int32)
    copy = pltpu.make_async_copy(row, origin, done)
    copy.start()
    force[...] = dot_t(pick, last)
    copy.wait()
    for j in range(SLOTS):
        held[pl.ds(j, LEV, stride=SLOTS), :] = main[pl.ds(origin[0, j] * SENT, LEV), :]

    def keep(first, count, stepped):
        out[first * SLOTS : (first + count) * SLOTS, :] = stepped

    run_cloud(held, force, table, middle, keep)


def next_kernel(dyn, inner, edge, out):
    me = lax.axis_index("mem")
    behind = lax.rem(me + N_MEM - 1, N_MEM)
    for y in range(ROWS):
        point = iota((POINTS, 2 * HALF), 0)
        left = edge[pl.ds(behind * ROWS + y, 1), :]
        right = edge[pl.ds(me * ROWS + y, 1), :]
        ratio = jnp.where(point == 0, left, jnp.where(point == POINTS - 1, right, inner[y]))
        out[0, y] = dyn[0, y] + 0.2 * ratio[:, :LEV]
        out[1, y] = dyn[1, y] + 0.2 * ratio[:, HALF : HALF + LEV]


def column_kernel(tendency, gathered, out):
    serves = gathered[:, :SLOTS, :].reshape(COLS, 2 * HALF)[:, LEV : LEV + 1]
    column = (iota((COLS, SLOTS), 1) + lax.axis_index("mem") * SLOTS).astype(F32)
    pick = jnp.where(serves == column, 1.0, 0.0).astype(F32)
    mine = dot_t(pick, tendency[...])
    out[0] = mine[:, :LEV]
    out[1] = mine[:, HALF : HALF + LEV]


def call(kernel, shapes, specs, scratch=(), out_specs=None, aliases=None, limit=24):
    many = isinstance(shapes, list)
    out = [jax.ShapeDtypeStruct(s, F32) for s in shapes] if many else jax.ShapeDtypeStruct(shapes, F32)
    return pl.pallas_call(
        kernel,
        out_shape=out,
        in_specs=specs,
        out_specs=out_specs or ([VMEM] * len(shapes) if many else VMEM),
        scratch_shapes=[pltpu.VMEM(s, F32) if isinstance(s, tuple) else s for s in scratch],
        input_output_aliases=aliases or {},
        compiler_params=pltpu.CompilerParams(vmem_limit_bytes=limit * 2**20),
    )


def on_device(dyn_state, wind_speed, mass_weight, crm_state, batch_map, sub_steps, migrate_to):
    lanes = 2 * HALF
    dyn = dyn_state.transpose(0, 2, 3, 1)
    wind = wind_speed.transpose(1, 2, 0)
    state = crm_state.transpose(1, 0, 2).reshape(LEV * SLOTS, lanes)
    batch, steps, moves = (a.reshape(1, SLOTS) for a in (batch_map, sub_steps, migrate_to))
    table = jnp.asarray(np.kron(np.eye(ROWS * POINTS // 4), derivative_table()).astype(np.float32))

    cells = LEV * SLOTS
    dma = pltpu.SemaphoreType.DMA
    ints = pltpu.VMEM((1, SLOTS), jnp.int32)
    weighed, top, end = call(
        weigh_kernel,
        [(ROWS, POINTS, lanes), (1, POINTS, lanes), (1, POINTS, lanes)],
        [HBM] * 5,
        [(2, ROWS, POINTS, LEV), (ROWS, POINTS, LEV), (ROWS, POINTS), table.shape, ints, dma((5,))],
        limit=60,
    )(dyn, wind, mass_weight, table, batch)
    weighed, state_later = lax.optimization_barrier((weighed, state))
    buckets = call(bucket_kernel, (N_GRP * SENT, lanes), [SMEM, VMEM])(migrate_to, state_later)
    up = [(i, (i + 1) % N_GRP) for i in range(N_GRP)]
    down = [(j, i) for i, j in up]
    before = lax.ppermute(end, "grp", up)
    after = lax.ppermute(top, "grp", down)
    inner, payload = call(
        assemble_kernel, [(ROWS, POINTS, lanes), (N_MEM, SLOTS + 2 * ROWS, lanes)], [VMEM] * 3
    )(weighed, before, after)
    gathered = lax.all_to_all(payload, "mem", 0, 0, tiled=True)
    force, edge, filled = call(
        forcing_kernel,
        [(SLOTS, lanes), (N_MEM * ROWS, lanes), (N_GRP, SENT, 1, lanes)],
        [VMEM] * 4 + [HBM],
        [(N_GRP, 1, lanes), dma],
        [VMEM, VMEM, HBM],
        {4: 2},
        limit=61,
    )(gathered, batch, moves, steps, buckets.reshape(N_GRP, SENT, 1, lanes))
    main = lax.all_to_all(filled, "grp", 0, 0, tiled=True)
    mix, means = jnp.asarray(neighbours_table()), jnp.asarray(means_table())
    tendency = call(tendency_kernel, (SLOTS, lanes), [VMEM] * 4, [(cells, lanes)])(state, force, mix, means)
    tendencies = lax.all_gather(tendency, "mem", axis=0, tiled=True)
    dyn_next = call(next_kernel, (2, ROWS, POINTS, LEV), [VMEM] * 3)(dyn, inner, edge)
    phys = call(column_kernel, (2, SLOTS, LEV), [VMEM] * 2)(tendencies, gathered)
    new = call(
        arrive_kernel,
        (cells, lanes),
        [VMEM] * 2,
        [(cells, lanes)] * 2
        + [(SLOTS, lanes), ints, pltpu.SMEM((1, SLOTS), jnp.int32), dma],
    )(main.reshape(N_GRP * SENT, lanes), mix)
    crm_next = new.reshape(LEV, SLOTS, lanes).transpose(1, 0, 2)
    return (dyn_next.transpose(0, 3, 1, 2), phys.transpose(0, 2, 1), crm_next)


def solution(mesh):
    placed = (
        P(None, None, "grp", "mem"),
        P(None, "grp", "mem"),
        P("grp", "mem"),
        P(("grp", "mem"), None, None),
        P(("grp", "mem")),
        P(("grp", "mem")),
        P(("grp", "mem")),
    )
    return jax.shard_map(
        on_device,
        mesh=mesh,
        in_specs=placed,
        out_specs=(
            P(None, None, "grp", "mem"),
            P(None, None, ("grp", "mem")),
            P(("grp", "mem"), None, None),
        ),
        check_vma=False,
    )
```

```python
import jax
import jax.numpy as jnp
import numpy as np
from jax import lax
from jax.experimental import pallas as pl
from jax.experimental.pallas import tpu as pltpu
from jax.sharding import PartitionSpec as P

NSUB = 2
LEV = 58
HALF = 64
SLOTS = 32
N_GRP = 64
N_MEM = 12
ROWS = 4
POINTS = 32
COLS = SLOTS * N_MEM
HIGH = lax.Precision.HIGHEST
VMEM = pl.BlockSpec(memory_space=pltpu.VMEM)
SMEM = pl.BlockSpec(memory_space=pltpu.SMEM)
HBM = pl.BlockSpec(memory_space=pltpu.HBM)
F32 = jnp.float32


def derivative_table():
    nodes = np.array([-1.0, -1.0 / np.sqrt(5.0), 1.0 / np.sqrt(5.0), 1.0])
    table = np.zeros((4, 4))
    for i in range(4):
        for j in range(4):
            if i == j:
                table[i, j] = sum(1.0 / (nodes[j] - nodes[k]) for k in range(4) if k != j)
            else:
                top = np.prod([nodes[i] - nodes[k] for k in range(4) if k not in (i, j)])
                low = np.prod([nodes[j] - nodes[k] for k in range(4) if k != j])
                table[i, j] = top / low
    return table.astype(np.float32)


def iota(shape, dim):
    return lax.broadcasted_iota(jnp.int32, shape, dim)


def dot(a, b):
    return jnp.dot(a, b, precision=HIGH, preferred_element_type=F32)


def dot_t(a, b):
    return lax.dot_general(a, b, (((0,), (0,)), ((), ())), precision=HIGH, preferred_element_type=F32)


def to_column(row):
    n = row.shape[1]
    return jnp.sum(jnp.where(iota((n, n), 0) == iota((n, n), 1), row, 0.0), axis=1, keepdims=True)


def both_kinds(heat, moist):
    gap = jnp.zeros((heat.shape[0], HALF - LEV), F32)
    return jnp.concatenate([heat, gap, moist, gap], axis=1)


def bucket_kernel(migrate, state, early, late):
    for s in range(SLOTS):
        group = lax.div(migrate[s], COLS)
        early[pl.ds(group * EARLY, EARLY), :] = state[pl.ds(s, EARLY, stride=SLOTS), :]
        late[pl.ds(group * SENT, LATE), :] = state[pl.ds(EARLY * SLOTS + s, LATE, stride=SLOTS), :]


def weigh_kernel(dyn_at, wind_at, mass_at, table_at, batch_at, out, top, end, dyn, wind, mass, table, batch, done):
    pairs = [(dyn_at, dyn), (wind_at, wind), (mass_at, mass), (table_at, table), (batch_at, batch)]
    copies = [pltpu.make_async_copy(a, b, done.at[i]) for i, (a, b) in enumerate(pairs)]
    for copy in copies:
        copy.start()
    for copy in copies:
        copy.wait()
    field = both_kinds(dyn[0].reshape(ROWS * POINTS, LEV), dyn[1].reshape(ROWS * POINTS, LEV))
    blow = wind[...].reshape(ROWS * POINTS, LEV)
    slope = dot(table[...], field)
    column = jnp.concatenate([to_column(mass[y : y + 1, :]) for y in range(ROWS)], axis=0)
    weighed = column * (-both_kinds(blow, blow) * slope)
    lane = iota((ROWS * POINTS, 2 * HALF), 1)
    serves = jnp.concatenate([to_column(batch[...].astype(F32))] * ROWS, axis=0)
    spare = jnp.where(lane == LEV, column, serves)
    weighed = jnp.where((lane == LEV) | (lane == LEV + 1), spare, weighed)
    weighed = weighed.reshape(ROWS, POINTS, 2 * HALF)
    out[...] = weighed
    top[0] = weighed[0]
    end[0] = weighed[ROWS - 1]


def assemble_kernel(own, before, after, inner, payload):
    rows = [own[0] + before[0], own[1], own[2], own[3] + after[0]]
    point = iota((POINTS, 2 * HALF), 0)
    means, edges = [], []
    for y, row in enumerate(rows):
        opening = (point % 4 == 0) & (point > 0)
        closing = (point % 4 == 3) & (point < POINTS - 1)
        full = (
            row
            + jnp.where(opening, pltpu.roll(row, 1, 0), 0.0)
            + jnp.where(closing, pltpu.roll(row, POINTS - 1, 0), 0.0)
        )
        ratio = full / full[:, LEV : LEV + 1]
        inner[y] = ratio
        means.append(jnp.where((point == 0) | (point == POINTS - 1), 0.0, ratio))
        edges.append(row)
    col, pt = iota((SLOTS, ROWS * POINTS), 0), iota((SLOTS, ROWS * POINTS), 1)
    inside = (col // 16 == pt // (2 * POINTS)) & (col % 16 == (pt % POINTS) // 2)
    average = jnp.where(inside, 0.25, 0.0).astype(F32)
    forcing = dot(average, jnp.concatenate(means, axis=0))
    left = [row[0:1] for row in edges]
    right = [row[POINTS - 1 : POINTS] for row in edges]
    lane = iota((SLOTS, 2 * HALF), 1)
    forcing = jnp.where(lane == LEV, own[0][:, LEV + 1 : LEV + 2], forcing)
    payload[...] = jnp.concatenate([forcing] + left + right, axis=0)


def forcing_kernel(gathered, batch, migrate, steps, late, force, edge, filled):
    rows = []
    for d in range(N_MEM):
        right = gathered[d, SLOTS + ROWS : SLOTS + 2 * ROWS, :]
        left = gathered[(d + 1) % N_MEM, SLOTS : SLOTS + ROWS, :]
        both = right + left
        rows.append(both / both[:, LEV : LEV + 1])
    joined = jnp.concatenate(rows, axis=0)
    edge[...] = joined
    columns = gathered[:, :SLOTS, :].reshape(COLS, 2 * HALF)
    slot = batch[...]
    pick = jnp.where(iota((COLS, SLOTS), 0) == slot, 1.0, 0.0).astype(F32)
    e = iota((N_MEM * ROWS, SLOTS), 0)
    dev, half = e // ROWS, (e % ROWS) // 2
    ahead = jnp.where(dev == N_MEM - 1, 0, dev + 1)
    last = slot == dev * SLOTS + half * 16 + 15
    first = slot == ahead * SLOTS + half * 16
    pick_edge = jnp.where(last, 0.25, 0.0) + jnp.where(first, 0.25, 0.0)
    forced = dot_t(pick, columns) + dot_t(pick_edge, joined)
    new = migrate[...]
    place = to_column((new & (SLOTS - 1)).astype(F32)) + 1.0
    count = to_column(steps[...].astype(F32))
    lane = iota((SLOTS, 2 * HALF), 1)
    forced = jnp.where(lane == LEV, place, jnp.where(lane == LEV + 1, count, forced))
    force[...] = forced
    group = jnp.floor((new.astype(F32) + 0.5) * (1.0 / COLS)).astype(jnp.int32)
    goes = jnp.where(iota((N_GRP, SLOTS), 0) == group, 1.0, 0.0).astype(F32)
    filled[...] = late[...]
    filled[pl.ds(LATE, N_GRP, stride=SENT), :] = dot(goes, forced)


def neighbours_table():
    lanes = 2 * HALF
    table = np.zeros((lanes, 2 * lanes))
    for base in (0, HALF):
        for c in range(HALF):
            table[base + (c + 1) % HALF, base + c] += 1.0
            table[base + (c - 1) % HALF, base + c] += 1.0
            table[c, lanes + base + c] -= 1.0
            table[HALF + c, lanes + base + c] += 1.0
    return np.concatenate([table, table], axis=0).astype(jnp.bfloat16)


def means_table():
    same = np.kron(np.eye(2), np.ones((HALF, HALF))) / HALF
    return np.concatenate([same, same], axis=0).astype(jnp.bfloat16)


def two_parts(value):
    lead = value.astype(jnp.bfloat16)
    trail = (value - lead.astype(F32)).astype(jnp.bfloat16)
    return jnp.concatenate([lead, trail], axis=1)


EARLY = 30
LATE = LEV - EARLY
SENT = LATE + 1
CHUNKS = [(0, 8), (8, 8), (16, 8), (24, 8), (32, 8), (40, 8), (48, 8), (56, 2)]


def substep(source, first, count, forced, active, table):
    rows = count * SLOTS
    at = lambda l, n: source[l * SLOTS : (l + n) * SLOTS, :]
    current = at(first, count)
    if first + count < LEV:
        upper = at(first + 1, count)
    else:
        upper = jnp.concatenate([at(first + 1, count - 1), at(LEV - 1, 1)], axis=0)
    if first > 0:
        lower = at(first - 1, count)
    else:
        lower = jnp.concatenate([at(0, 1), at(0, count - 1)], axis=0)
    mixed = jnp.dot(two_parts(current), table, preferred_element_type=F32)
    side, gap = mixed[:, : 2 * HALF], mixed[:, 2 * HALF :]
    soft = jnp.maximum(gap, 0.0) + jnp.log(1.0 + jnp.exp(-jnp.abs(gap)))
    sign = jnp.where(iota((rows, 2 * HALF), 1) < HALF, 0.05, -0.1)
    updated = 0.5 * current + forced + 0.15 * side + 0.1 * (upper + lower) + sign * soft
    on = jnp.broadcast_to(active, (SLOTS, 2 * HALF))
    return jnp.where(jnp.concatenate([on] * count, axis=0), updated, current)


def spread(quarter, first, count):
    lane = iota((SLOTS, 2 * HALF), 1)
    return jnp.concatenate(
        [
            jnp.take_along_axis(quarter, (lane & HALF) + level, axis=1, mode="promise_in_bounds")
            for level in range(first, first + count)
        ],
        axis=0,
    )


def run_cloud(state, force, table, middle, keep):
    steps = force[:, LEV + 1 : LEV + 2]
    quarter = 0.25 * force[...]
    for first, count in CHUNKS:
        forced = spread(quarter, first, count)
        rows = pl.ds(first * SLOTS, count * SLOTS)
        middle[rows, :] = substep(state, first, count, forced, steps > 0.5, table[...])
    for first, count in CHUNKS:
        forced = spread(quarter, first, count)
        keep(first, count, substep(middle, first, count, forced, steps > 1.5, table[...]))


def tendency_kernel(state, force, table, means, send, middle):
    column = iota((SLOTS, 2 * HALF), 1) & (HALF - 1)
    send[...] = jnp.zeros((SLOTS, 2 * HALF), F32)

    def keep(first, count, stepped):
        change = stepped - state[first * SLOTS : (first + count) * SLOTS, :]
        mean = jnp.dot(two_parts(change), means[...], preferred_element_type=F32)
        total = send[...]
        for i in range(count):
            total = jnp.where(column == first + i, mean[i * SLOTS : (i + 1) * SLOTS, :], total)
        send[...] = total

    run_cloud(state, force, table, middle, keep)


def arrive_kernel(early, late, table, out, held, middle, force, row, origin, done):
    last = late[pl.ds(LATE, N_GRP, stride=SENT), :]
    slot = (iota((N_GRP, SLOTS), 1) + 1).astype(F32)
    pick = jnp.where(last[:, LEV : LEV + 1] == slot, 1.0, 0.0).astype(F32)
    group = iota((N_GRP, SLOTS), 0).astype(F32)
    row[...] = jnp.sum(pick * group, axis=0, keepdims=True).astype(jnp.int32)
    copy = pltpu.make_async_copy(row, origin, done)
    copy.start()
    force[...] = dot_t(pick, last)
    copy.wait()
    for j in range(SLOTS):
        g = origin[0, j]
        held[pl.ds(j, EARLY, stride=SLOTS), :] = early[pl.ds(g * EARLY, EARLY), :]
        held[pl.ds(EARLY * SLOTS + j, LATE, stride=SLOTS), :] = late[pl.ds(g * SENT, LATE), :]

    def keep(first, count, stepped):
        out[first * SLOTS : (first + count) * SLOTS, :] = stepped

    run_cloud(held, force, table, middle, keep)


def next_kernel(dyn, inner, edge, out):
    me = lax.axis_index("mem")
    behind = lax.rem(me + N_MEM - 1, N_MEM)
    for y in range(ROWS):
        point = iota((POINTS, 2 * HALF), 0)
        left = edge[pl.ds(behind * ROWS + y, 1), :]
        right = edge[pl.ds(me * ROWS + y, 1), :]
        ratio = jnp.where(point == 0, left, jnp.where(point == POINTS - 1, right, inner[y]))
        out[0, y] = dyn[0, y] + 0.2 * ratio[:, :LEV]
        out[1, y] = dyn[1, y] + 0.2 * ratio[:, HALF : HALF + LEV]


def column_kernel(tendency, gathered, out):
    serves = gathered[:, :SLOTS, :].reshape(COLS, 2 * HALF)[:, LEV : LEV + 1]
    column = (iota((COLS, SLOTS), 1) + lax.axis_index("mem") * SLOTS).astype(F32)
    pick = jnp.where(serves == column, 1.0, 0.0).astype(F32)
    mine = dot_t(pick, tendency[...])
    out[0] = mine[:, :LEV]
    out[1] = mine[:, HALF : HALF + LEV]


def call(kernel, shapes, specs, scratch=(), out_specs=None, aliases=None, limit=24):
    many = isinstance(shapes, list)
    out = [jax.ShapeDtypeStruct(s, F32) for s in shapes] if many else jax.ShapeDtypeStruct(shapes, F32)
    return pl.pallas_call(
        kernel,
        out_shape=out,
        in_specs=specs,
        out_specs=out_specs or ([VMEM] * len(shapes) if many else VMEM),
        scratch_shapes=[pltpu.VMEM(s, F32) if isinstance(s, tuple) else s for s in scratch],
        input_output_aliases=aliases or {},
        compiler_params=pltpu.CompilerParams(vmem_limit_bytes=limit * 2**20),
    )


def on_device(dyn_state, wind_speed, mass_weight, crm_state, batch_map, sub_steps, migrate_to):
    lanes = 2 * HALF
    dyn = dyn_state.transpose(0, 2, 3, 1)
    wind = wind_speed.transpose(1, 2, 0)
    state = crm_state.transpose(1, 0, 2).reshape(LEV * SLOTS, lanes)
    batch, steps, moves = (a.reshape(1, SLOTS) for a in (batch_map, sub_steps, migrate_to))
    table = jnp.asarray(np.kron(np.eye(ROWS * POINTS // 4), derivative_table()).astype(np.float32))

    cells = LEV * SLOTS
    dma = pltpu.SemaphoreType.DMA
    ints = pltpu.VMEM((1, SLOTS), jnp.int32)
    weighed, top, end = call(
        weigh_kernel,
        [(ROWS, POINTS, lanes), (1, POINTS, lanes), (1, POINTS, lanes)],
        [HBM] * 5,
        [(2, ROWS, POINTS, LEV), (ROWS, POINTS, LEV), (ROWS, POINTS), table.shape, ints, dma((5,))],
        limit=60,
    )(dyn, wind, mass_weight, table, batch)
    weighed, state_later = lax.optimization_barrier((weighed, state))
    early, late = call(bucket_kernel, [(N_GRP * EARLY, lanes), (N_GRP * SENT, lanes)], [SMEM, VMEM])(
        migrate_to, state_later
    )
    up = [(i, (i + 1) % N_GRP) for i in range(N_GRP)]
    down = [(j, i) for i, j in up]
    before = lax.ppermute(end, "grp", up)
    after = lax.ppermute(top, "grp", down)
    early, before, after = lax.optimization_barrier((early, before, after))
    first = lax.all_to_all(early.reshape(N_GRP, EARLY, 1, lanes), "grp", 0, 0, tiled=True)
    inner, payload = call(
        assemble_kernel, [(ROWS, POINTS, lanes), (SLOTS + 2 * ROWS, lanes)], [VMEM] * 3
    )(weighed, before, after)
    gathered = lax.all_gather(payload, "mem", axis=0)
    force, edge, filled = call(
        forcing_kernel,
        [(SLOTS, lanes), (N_MEM * ROWS, lanes), (N_GRP * SENT, lanes)],
        [VMEM] * 5,
    )(gathered, batch, moves, steps, late)
    filled, first = lax.optimization_barrier((filled, first))
    second = lax.all_to_all(filled.reshape(N_GRP, SENT, 1, lanes), "grp", 0, 0, tiled=True)
    mix, means = jnp.asarray(neighbours_table()), jnp.asarray(means_table())
    tendency = call(tendency_kernel, (SLOTS, lanes), [VMEM] * 4, [(cells, lanes)])(state, force, mix, means)
    tendencies = lax.all_gather(tendency, "mem", axis=0, tiled=True)
    dyn_next = call(next_kernel, (2, ROWS, POINTS, LEV), [VMEM] * 3)(dyn, inner, edge)
    phys = call(column_kernel, (2, SLOTS, LEV), [VMEM] * 2)(tendencies, gathered)
    new = call(
        arrive_kernel,
        (cells, lanes),
        [VMEM] * 3,
        [(cells, lanes)] * 2
        + [(SLOTS, lanes), ints, pltpu.SMEM((1, SLOTS), jnp.int32), dma],
    )(first.reshape(N_GRP * EARLY, lanes), second.reshape(N_GRP * SENT, lanes), mix)
    crm_next = new.reshape(LEV, SLOTS, lanes).transpose(1, 0, 2)
    return (dyn_next.transpose(0, 3, 1, 2), phys.transpose(0, 2, 1), crm_next)


def solution(mesh):
    placed = (
        P(None, None, "grp", "mem"),
        P(None, "grp", "mem"),
        P("grp", "mem"),
        P(("grp", "mem"), None, None),
        P(("grp", "mem")),
        P(("grp", "mem")),
        P(("grp", "mem")),
    )
    return jax.shard_map(
        on_device,
        mesh=mesh,
        in_specs=placed,
        out_specs=(
            P(None, None, "grp", "mem"),
            P(None, None, ("grp", "mem")),
            P(("grp", "mem"), None, None),
        ),
        check_vma=False,
    )
```

```python
import jax
import jax.numpy as jnp
import numpy as np
from jax import lax
from jax.experimental import pallas as pl
from jax.experimental.pallas import tpu as pltpu
from jax.sharding import PartitionSpec as P

NSUB = 2
LEV = 58
HALF = 64
SLOTS = 32
N_GRP = 64
N_MEM = 12
ROWS = 4
POINTS = 32
COLS = SLOTS * N_MEM
HIGH = lax.Precision.HIGHEST
VMEM = pl.BlockSpec(memory_space=pltpu.VMEM)
SMEM = pl.BlockSpec(memory_space=pltpu.SMEM)
HBM = pl.BlockSpec(memory_space=pltpu.HBM)
F32 = jnp.float32


def derivative_table():
    nodes = np.array([-1.0, -1.0 / np.sqrt(5.0), 1.0 / np.sqrt(5.0), 1.0])
    table = np.zeros((4, 4))
    for i in range(4):
        for j in range(4):
            if i == j:
                table[i, j] = sum(1.0 / (nodes[j] - nodes[k]) for k in range(4) if k != j)
            else:
                top = np.prod([nodes[i] - nodes[k] for k in range(4) if k not in (i, j)])
                low = np.prod([nodes[j] - nodes[k] for k in range(4) if k != j])
                table[i, j] = top / low
    return table.astype(np.float32)


def iota(shape, dim):
    return lax.broadcasted_iota(jnp.int32, shape, dim)


def dot(a, b):
    return jnp.dot(a, b, precision=HIGH, preferred_element_type=F32)


def dot_t(a, b):
    return lax.dot_general(a, b, (((0,), (0,)), ((), ())), precision=HIGH, preferred_element_type=F32)


def to_column(row):
    n = row.shape[1]
    return jnp.sum(jnp.where(iota((n, n), 0) == iota((n, n), 1), row, 0.0), axis=1, keepdims=True)


def both_kinds(heat, moist):
    gap = jnp.zeros((heat.shape[0], HALF - LEV), F32)
    return jnp.concatenate([heat, gap, moist, gap], axis=1)


def bucket_kernel(migrate, state, batch, moves, steps, early, late, index):
    new = moves[...]
    group = jnp.floor((new.astype(F32) + 0.5) * (1.0 / COLS))
    place = (new & (SLOTS - 1)).astype(F32) + 1.0
    lane = iota((SLOTS, 2 * HALF), 1)
    columns = jnp.zeros((SLOTS, 2 * HALF), F32)
    for i, row in enumerate((batch[...].astype(F32), place, steps[...].astype(F32), group)):
        columns = jnp.where(lane == i, to_column(row), columns)
    index[...] = columns
    for s in range(SLOTS):
        group = lax.div(migrate[s], COLS)
        early[pl.ds(pl.multiple_of(group * EARLY, 8), EARLY), :] = state[pl.ds(s, EARLY, stride=SLOTS), :]
        late[pl.ds(group * SENT, LATE), :] = state[pl.ds(EARLY * SLOTS + s, LATE, stride=SLOTS), :]


def weigh_kernel(dyn_at, wind_at, mass_at, table_at, batch_at, out, top, end, dyn, wind, mass, table, batch, done):
    pairs = [(dyn_at, dyn), (wind_at, wind), (mass_at, mass), (table_at, table), (batch_at, batch)]
    copies = [pltpu.make_async_copy(a, b, done.at[i]) for i, (a, b) in enumerate(pairs)]
    for copy in copies:
        copy.start()
    for copy in copies:
        copy.wait()
    field = both_kinds(dyn[0].reshape(ROWS * POINTS, LEV), dyn[1].reshape(ROWS * POINTS, LEV))
    blow = wind[...].reshape(ROWS * POINTS, LEV)
    slope = dot(table[...], field)
    column = jnp.concatenate([to_column(mass[y : y + 1, :]) for y in range(ROWS)], axis=0)
    weighed = column * (-both_kinds(blow, blow) * slope)
    lane = iota((ROWS * POINTS, 2 * HALF), 1)
    serves = jnp.concatenate([to_column(batch[...].astype(F32))] * ROWS, axis=0)
    spare = jnp.where(lane == LEV, column, serves)
    weighed = jnp.where((lane == LEV) | (lane == LEV + 1), spare, weighed)
    weighed = weighed.reshape(ROWS, POINTS, 2 * HALF)
    out[...] = weighed
    top[0] = weighed[0]
    end[0] = weighed[ROWS - 1]


def assemble_kernel(own, before, after, inner, payload):
    rows = [own[0] + before[0], own[1], own[2], own[3] + after[0]]
    point = iota((POINTS, 2 * HALF), 0)
    means, edges = [], []
    for y, row in enumerate(rows):
        opening = (point % 4 == 0) & (point > 0)
        closing = (point % 4 == 3) & (point < POINTS - 1)
        full = (
            row
            + jnp.where(opening, pltpu.roll(row, 1, 0), 0.0)
            + jnp.where(closing, pltpu.roll(row, POINTS - 1, 0), 0.0)
        )
        ratio = full / full[:, LEV : LEV + 1]
        inner[y] = ratio
        means.append(jnp.where((point == 0) | (point == POINTS - 1), 0.0, ratio))
        edges.append(row)
    col, pt = iota((SLOTS, ROWS * POINTS), 0), iota((SLOTS, ROWS * POINTS), 1)
    inside = (col // 16 == pt // (2 * POINTS)) & (col % 16 == (pt % POINTS) // 2)
    average = jnp.where(inside, 0.25, 0.0).astype(F32)
    forcing = dot(average, jnp.concatenate(means, axis=0))
    left = [row[0:1] for row in edges]
    right = [row[POINTS - 1 : POINTS] for row in edges]
    lane = iota((SLOTS, 2 * HALF), 1)
    forcing = jnp.where(lane == LEV, own[0][:, LEV + 1 : LEV + 2], forcing)
    payload[...] = jnp.concatenate([forcing] + left + right, axis=0)


def forcing_kernel(gathered, index, late, force, edge, filled):
    rows = []
    for d in range(N_MEM):
        right = gathered[d, SLOTS + ROWS : SLOTS + 2 * ROWS, :]
        left = gathered[(d + 1) % N_MEM, SLOTS : SLOTS + ROWS, :]
        both = right + left
        rows.append(both / both[:, LEV : LEV + 1])
    joined = jnp.concatenate(rows, axis=0)
    edge[...] = joined
    columns = gathered[:, :SLOTS, :].reshape(COLS, 2 * HALF)
    slot = index[:, 0:1].astype(jnp.int32)
    pick = jnp.where(iota((SLOTS, COLS), 1) == slot, 1.0, 0.0).astype(F32)
    e = iota((SLOTS, N_MEM * ROWS), 1)
    dev, half = e // ROWS, (e % ROWS) // 2
    ahead = jnp.where(dev == N_MEM - 1, 0, dev + 1)
    last = slot == dev * SLOTS + half * 16 + 15
    first = slot == ahead * SLOTS + half * 16
    pick_edge = jnp.where(last, 0.25, 0.0) + jnp.where(first, 0.25, 0.0)
    forced = dot(pick, columns) + dot(pick_edge, joined)
    lane = iota((SLOTS, 2 * HALF), 1)
    forced = jnp.where(lane == LEV, index[:, 1:2], jnp.where(lane == LEV + 1, index[:, 2:3], forced))
    force[...] = forced
    goes = jnp.where(iota((SLOTS, N_GRP), 1) == index[:, 3:4].astype(jnp.int32), 1.0, 0.0).astype(F32)
    filled[...] = late[...]
    filled[pl.ds(LATE, N_GRP, stride=SENT), :] = dot_t(goes, forced)


def neighbours_table():
    lanes = 2 * HALF
    table = np.zeros((lanes, 2 * lanes))
    for base in (0, HALF):
        for c in range(HALF):
            table[base + (c + 1) % HALF, base + c] += 1.0
            table[base + (c - 1) % HALF, base + c] += 1.0
            table[c, lanes + base + c] -= 1.0
            table[HALF + c, lanes + base + c] += 1.0
    return np.concatenate([table, table], axis=0).astype(jnp.bfloat16)


def means_table():
    same = np.kron(np.eye(2), np.ones((HALF, HALF))) / HALF
    return np.concatenate([same, same], axis=0).astype(jnp.bfloat16)


def two_parts(value):
    lead = value.astype(jnp.bfloat16)
    trail = (value - lead.astype(F32)).astype(jnp.bfloat16)
    return jnp.concatenate([lead, trail], axis=1)


EARLY = 32
LATE = LEV - EARLY
SENT = LATE + 1
CHUNKS = [(0, 8), (8, 8), (16, 8), (24, 8), (32, 8), (40, 8), (48, 8), (56, 2)]


def substep(source, first, count, forced, active, table):
    rows = count * SLOTS
    at = lambda l, n: source[l * SLOTS : (l + n) * SLOTS, :]
    current = at(first, count)
    if first + count < LEV:
        upper = at(first + 1, count)
    else:
        upper = jnp.concatenate([at(first + 1, count - 1), at(LEV - 1, 1)], axis=0)
    if first > 0:
        lower = at(first - 1, count)
    else:
        lower = jnp.concatenate([at(0, 1), at(0, count - 1)], axis=0)
    mixed = jnp.dot(two_parts(current), table, preferred_element_type=F32)
    side, gap = mixed[:, : 2 * HALF], mixed[:, 2 * HALF :]
    soft = jnp.maximum(gap, 0.0) + jnp.log(1.0 + jnp.exp(-jnp.abs(gap)))
    sign = jnp.where(iota((rows, 2 * HALF), 1) < HALF, 0.05, -0.1)
    updated = 0.5 * current + forced + 0.15 * side + 0.1 * (upper + lower) + sign * soft
    on = jnp.broadcast_to(active, (SLOTS, 2 * HALF))
    return jnp.where(jnp.concatenate([on] * count, axis=0), updated, current)


def spread(quarter, first, count):
    lane = iota((SLOTS, 2 * HALF), 1)
    return jnp.concatenate(
        [
            jnp.take_along_axis(quarter, (lane & HALF) + level, axis=1, mode="promise_in_bounds")
            for level in range(first, first + count)
        ],
        axis=0,
    )


def run_cloud(state, force, table, middle, keep):
    steps = force[:, LEV + 1 : LEV + 2]
    quarter = 0.25 * force[...]
    for first, count in CHUNKS:
        forced = spread(quarter, first, count)
        rows = pl.ds(first * SLOTS, count * SLOTS)
        middle[rows, :] = substep(state, first, count, forced, steps > 0.5, table[...])
    for first, count in CHUNKS:
        forced = spread(quarter, first, count)
        keep(first, count, substep(middle, first, count, forced, steps > 1.5, table[...]))


def tendency_kernel(state, force, table, means, send, middle):
    column = iota((SLOTS, 2 * HALF), 1) & (HALF - 1)
    send[...] = jnp.zeros((SLOTS, 2 * HALF), F32)

    def keep(first, count, stepped):
        change = stepped - state[first * SLOTS : (first + count) * SLOTS, :]
        mean = jnp.dot(two_parts(change), means[...], preferred_element_type=F32)
        total = send[...]
        for i in range(count):
            total = jnp.where(column == first + i, mean[i * SLOTS : (i + 1) * SLOTS, :], total)
        send[...] = total

    run_cloud(state, force, table, middle, keep)


def arrive_kernel(early, late, table, out, held, middle, stepped_at, force, row, origin, done, written):
    last = late[pl.ds(LATE, N_GRP, stride=SENT), :]
    slot = (iota((N_GRP, SLOTS), 1) + 1).astype(F32)
    pick = jnp.where(last[:, LEV : LEV + 1] == slot, 1.0, 0.0).astype(F32)
    group = iota((N_GRP, SLOTS), 0).astype(F32)
    row[...] = jnp.sum(pick * group, axis=0, keepdims=True).astype(jnp.int32)
    copy = pltpu.make_async_copy(row, origin, done)
    copy.start()
    force[...] = dot_t(pick, last)
    copy.wait()
    for j in range(SLOTS):
        g = origin[0, j]
        held[pl.ds(j, EARLY, stride=SLOTS), :] = early[pl.ds(pl.multiple_of(g * EARLY, 8), EARLY), :]
        held[pl.ds(EARLY * SLOTS + j, LATE, stride=SLOTS), :] = late[pl.ds(g * SENT, LATE), :]

    copies = []

    def keep(first, count, stepped):
        rows = pl.ds(first * SLOTS, count * SLOTS)
        stepped_at[rows, :] = stepped
        copies.append(pltpu.make_async_copy(stepped_at.at[rows], out.at[rows], written.at[len(copies)]))
        copies[-1].start()

    run_cloud(held, force, table, middle, keep)
    for copy in copies:
        copy.wait()


def next_kernel(dyn, inner, edge, out):
    me = lax.axis_index("mem")
    behind = lax.rem(me + N_MEM - 1, N_MEM)
    for y in range(ROWS):
        point = iota((POINTS, 2 * HALF), 0)
        left = edge[pl.ds(behind * ROWS + y, 1), :]
        right = edge[pl.ds(me * ROWS + y, 1), :]
        ratio = jnp.where(point == 0, left, jnp.where(point == POINTS - 1, right, inner[y]))
        out[0, y] = dyn[0, y] + 0.2 * ratio[:, :LEV]
        out[1, y] = dyn[1, y] + 0.2 * ratio[:, HALF : HALF + LEV]


def column_kernel(tendency, gathered, out):
    serves = gathered[:, :SLOTS, :].reshape(COLS, 2 * HALF)[:, LEV : LEV + 1]
    column = (iota((COLS, SLOTS), 1) + lax.axis_index("mem") * SLOTS).astype(F32)
    pick = jnp.where(serves == column, 1.0, 0.0).astype(F32)
    mine = dot_t(pick, tendency[...])
    out[0] = mine[:, :LEV]
    out[1] = mine[:, HALF : HALF + LEV]


def call(kernel, shapes, specs, scratch=(), out_specs=None, aliases=None, limit=24):
    many = isinstance(shapes, list)
    out = [jax.ShapeDtypeStruct(s, F32) for s in shapes] if many else jax.ShapeDtypeStruct(shapes, F32)
    return pl.pallas_call(
        kernel,
        out_shape=out,
        in_specs=specs,
        out_specs=out_specs or ([VMEM] * len(shapes) if many else VMEM),
        scratch_shapes=[pltpu.VMEM(s, F32) if isinstance(s, tuple) else s for s in scratch],
        input_output_aliases=aliases or {},
        compiler_params=pltpu.CompilerParams(vmem_limit_bytes=limit * 2**20),
    )


def on_device(dyn_state, wind_speed, mass_weight, crm_state, batch_map, sub_steps, migrate_to):
    lanes = 2 * HALF
    dyn = dyn_state.transpose(0, 2, 3, 1)
    wind = wind_speed.transpose(1, 2, 0)
    state = crm_state.transpose(1, 0, 2).reshape(LEV * SLOTS, lanes)
    batch, steps, moves = (a.reshape(1, SLOTS) for a in (batch_map, sub_steps, migrate_to))
    table = jnp.asarray(np.kron(np.eye(ROWS * POINTS // 4), derivative_table()).astype(np.float32))

    cells = LEV * SLOTS
    dma = pltpu.SemaphoreType.DMA
    ints = pltpu.VMEM((1, SLOTS), jnp.int32)
    weighed, top, end = call(
        weigh_kernel,
        [(ROWS, POINTS, lanes), (1, POINTS, lanes), (1, POINTS, lanes)],
        [HBM] * 5,
        [(2, ROWS, POINTS, LEV), (ROWS, POINTS, LEV), (ROWS, POINTS), table.shape, ints, dma((5,))],
        limit=60,
    )(dyn, wind, mass_weight, table, batch)
    weighed, batch_later = lax.optimization_barrier((weighed, batch))
    early, late, index = call(
        bucket_kernel, [(N_GRP * EARLY, lanes), (N_GRP * SENT, lanes), (SLOTS, lanes)], [SMEM] + [VMEM] * 4
    )(migrate_to, state, batch_later, moves, steps)
    up = [(i, (i + 1) % N_GRP) for i in range(N_GRP)]
    down = [(j, i) for i, j in up]
    before = lax.ppermute(end, "grp", up)
    after = lax.ppermute(top, "grp", down)
    early, before, after = lax.optimization_barrier((early, before, after))
    first = lax.all_to_all(early.reshape(N_GRP, EARLY, 1, lanes), "grp", 0, 0, tiled=True)
    inner, payload = call(
        assemble_kernel, [(ROWS, POINTS, lanes), (SLOTS + 2 * ROWS, lanes)], [VMEM] * 3
    )(weighed, before, after)
    gathered = lax.all_gather(payload, "mem", axis=0)
    force, edge, filled = call(
        forcing_kernel,
        [(SLOTS, lanes), (N_MEM * ROWS, lanes), (N_GRP * SENT, lanes)],
        [VMEM] * 3,
    )(gathered, index, late)
    filled, first = lax.optimization_barrier((filled, first))
    second = lax.all_to_all(filled.reshape(N_GRP, SENT, 1, lanes), "grp", 0, 0, tiled=True)
    mix, means = jnp.asarray(neighbours_table()), jnp.asarray(means_table())
    tendency = call(tendency_kernel, (SLOTS, lanes), [VMEM] * 4, [(cells, lanes)])(state, force, mix, means)
    tendencies = lax.all_gather(tendency, "mem", axis=0, tiled=True)
    dyn_next = call(next_kernel, (2, ROWS, POINTS, LEV), [VMEM] * 3)(dyn, inner, edge)
    phys = call(column_kernel, (2, SLOTS, LEV), [VMEM] * 2)(tendencies, gathered)
    new = call(
        arrive_kernel,
        (cells, lanes),
        [VMEM] * 3,
        [(cells, lanes)] * 3
        + [(SLOTS, lanes), ints, pltpu.SMEM((1, SLOTS), jnp.int32), dma, dma((len(CHUNKS),))],
        HBM,
    )(first.reshape(N_GRP * EARLY, lanes), second.reshape(N_GRP * SENT, lanes), mix)
    crm_next = new.reshape(LEV, SLOTS, lanes).transpose(1, 0, 2)
    return (dyn_next.transpose(0, 3, 1, 2), phys.transpose(0, 2, 1), crm_next)


def solution(mesh):
    placed = (
        P(None, None, "grp", "mem"),
        P(None, "grp", "mem"),
        P("grp", "mem"),
        P(("grp", "mem"), None, None),
        P(("grp", "mem")),
        P(("grp", "mem")),
        P(("grp", "mem")),
    )
    return jax.shard_map(
        on_device,
        mesh=mesh,
        in_specs=placed,
        out_specs=(
            P(None, None, "grp", "mem"),
            P(None, None, ("grp", "mem")),
            P(("grp", "mem"), None, None),
        ),
        check_vma=False,
    )
```

```python
import jax
import jax.numpy as jnp
import numpy as np
from jax import lax
from jax.experimental import pallas as pl
from jax.experimental.pallas import tpu as pltpu
from jax.sharding import PartitionSpec as P

NSUB = 2
LEV = 58
HALF = 64
SLOTS = 32
N_GRP = 64
N_MEM = 12
ROWS = 4
POINTS = 32
COLS = SLOTS * N_MEM
HIGH = lax.Precision.HIGHEST
VMEM = pl.BlockSpec(memory_space=pltpu.VMEM)
SMEM = pl.BlockSpec(memory_space=pltpu.SMEM)
HBM = pl.BlockSpec(memory_space=pltpu.HBM)
F32 = jnp.float32


def derivative_table():
    nodes = np.array([-1.0, -1.0 / np.sqrt(5.0), 1.0 / np.sqrt(5.0), 1.0])
    table = np.zeros((4, 4))
    for i in range(4):
        for j in range(4):
            if i == j:
                table[i, j] = sum(1.0 / (nodes[j] - nodes[k]) for k in range(4) if k != j)
            else:
                top = np.prod([nodes[i] - nodes[k] for k in range(4) if k not in (i, j)])
                low = np.prod([nodes[j] - nodes[k] for k in range(4) if k != j])
                table[i, j] = top / low
    return table.astype(np.float32)


def iota(shape, dim):
    return lax.broadcasted_iota(jnp.int32, shape, dim)


def dot(a, b):
    return jnp.dot(a, b, precision=HIGH, preferred_element_type=F32)


def dot_t(a, b):
    return lax.dot_general(a, b, (((0,), (0,)), ((), ())), precision=HIGH, preferred_element_type=F32)


def to_column(row):
    n = row.shape[1]
    return jnp.sum(jnp.where(iota((n, n), 0) == iota((n, n), 1), row, 0.0), axis=1, keepdims=True)


def both_kinds(heat, moist):
    gap = jnp.zeros((heat.shape[0], HALF - LEV), F32)
    return jnp.concatenate([heat, gap, moist, gap], axis=1)


def index_columns(batch, moves, steps):
    new = moves[...]
    group = jnp.floor((new.astype(F32) + 0.5) * (1.0 / COLS))
    place = (new & (SLOTS - 1)).astype(F32) + 1.0
    lane = iota((SLOTS, 2 * HALF), 1)
    columns = jnp.zeros((SLOTS, 2 * HALF), F32)
    for i, row in enumerate((batch[...].astype(F32), place, steps[...].astype(F32), group)):
        columns = jnp.where(lane == i, to_column(row), columns)
    return columns


def first_kernel(*refs):
    given, (out, top, end, index, early_at, late_at) = refs[:9], refs[9:15]
    state, migrate, dyn, wind, mass, table, batch, moves, steps, early, late, done, sent = refs[15:]
    held = (state, migrate, dyn, wind, mass, table, batch, moves, steps)
    copies = [pltpu.make_async_copy(a, b, done.at[i]) for i, (a, b) in enumerate(zip(given, held))]
    for copy in copies:
        copy.start()
    for copy in copies:
        copy.wait()
    for s in range(SLOTS):
        group = lax.div(migrate[0, s], COLS)
        early[pl.ds(pl.multiple_of(group * EARLY, 8), EARLY), :] = state[pl.ds(s, EARLY, stride=SLOTS), :]
        late[pl.ds(group * SENT, LATE), :] = state[pl.ds(EARLY * SLOTS + s, LATE, stride=SLOTS), :]
    leaving = [
        pltpu.make_async_copy(early, early_at, sent.at[0]),
        pltpu.make_async_copy(late, late_at, sent.at[1]),
    ]
    for copy in leaving:
        copy.start()
    index[...] = index_columns(batch, moves, steps)
    field = both_kinds(dyn[0].reshape(ROWS * POINTS, LEV), dyn[1].reshape(ROWS * POINTS, LEV))
    blow = wind[...].reshape(ROWS * POINTS, LEV)
    slope = dot(table[...], field)
    column = jnp.concatenate([to_column(mass[y : y + 1, :]) for y in range(ROWS)], axis=0)
    weighed = column * (-both_kinds(blow, blow) * slope)
    lane = iota((ROWS * POINTS, 2 * HALF), 1)
    serves = jnp.concatenate([to_column(batch[...].astype(F32))] * ROWS, axis=0)
    spare = jnp.where(lane == LEV, column, serves)
    weighed = jnp.where((lane == LEV) | (lane == LEV + 1), spare, weighed)
    weighed = weighed.reshape(ROWS, POINTS, 2 * HALF)
    out[...] = weighed
    top[0] = weighed[0]
    end[0] = weighed[ROWS - 1]
    for copy in leaving:
        copy.wait()


def assemble_kernel(own, before, after, inner, payload):
    rows = [own[0] + before[0], own[1], own[2], own[3] + after[0]]
    point = iota((POINTS, 2 * HALF), 0)
    means, edges = [], []
    for y, row in enumerate(rows):
        opening = (point % 4 == 0) & (point > 0)
        closing = (point % 4 == 3) & (point < POINTS - 1)
        full = (
            row
            + jnp.where(opening, pltpu.roll(row, 1, 0), 0.0)
            + jnp.where(closing, pltpu.roll(row, POINTS - 1, 0), 0.0)
        )
        ratio = full / full[:, LEV : LEV + 1]
        inner[y] = ratio
        means.append(jnp.where((point == 0) | (point == POINTS - 1), 0.0, ratio))
        edges.append(row)
    col, pt = iota((SLOTS, ROWS * POINTS), 0), iota((SLOTS, ROWS * POINTS), 1)
    inside = (col // 16 == pt // (2 * POINTS)) & (col % 16 == (pt % POINTS) // 2)
    average = jnp.where(inside, 0.25, 0.0).astype(F32)
    forcing = dot(average, jnp.concatenate(means, axis=0))
    left = [row[0:1] for row in edges]
    right = [row[POINTS - 1 : POINTS] for row in edges]
    lane = iota((SLOTS, 2 * HALF), 1)
    forcing = jnp.where(lane == LEV, own[0][:, LEV + 1 : LEV + 2], forcing)
    payload[...] = jnp.concatenate([forcing] + left + right, axis=0)


def forcing_kernel(gathered, index, late, force, edge, filled):
    rows = []
    for d in range(N_MEM):
        right = gathered[d, SLOTS + ROWS : SLOTS + 2 * ROWS, :]
        left = gathered[(d + 1) % N_MEM, SLOTS : SLOTS + ROWS, :]
        both = right + left
        rows.append(both / both[:, LEV : LEV + 1])
    joined = jnp.concatenate(rows, axis=0)
    edge[...] = joined
    columns = gathered[:, :SLOTS, :].reshape(COLS, 2 * HALF)
    slot = index[:, 0:1].astype(jnp.int32)
    pick = jnp.where(iota((SLOTS, COLS), 1) == slot, 1.0, 0.0).astype(F32)
    e = iota((SLOTS, N_MEM * ROWS), 1)
    dev, half = e // ROWS, (e % ROWS) // 2
    ahead = jnp.where(dev == N_MEM - 1, 0, dev + 1)
    last = slot == dev * SLOTS + half * 16 + 15
    first = slot == ahead * SLOTS + half * 16
    pick_edge = jnp.where(last, 0.25, 0.0) + jnp.where(first, 0.25, 0.0)
    forced = dot(pick, columns) + dot(pick_edge, joined)
    lane = iota((SLOTS, 2 * HALF), 1)
    forced = jnp.where(lane == LEV, index[:, 1:2], jnp.where(lane == LEV + 1, index[:, 2:3], forced))
    force[...] = forced
    goes = jnp.where(iota((SLOTS, N_GRP), 1) == index[:, 3:4].astype(jnp.int32), 1.0, 0.0).astype(F32)
    filled[...] = late[...]
    filled[pl.ds(LATE, N_GRP, stride=SENT), :] = dot_t(goes, forced)


def neighbours_table():
    lanes = 2 * HALF
    table = np.zeros((lanes, 2 * lanes))
    for base in (0, HALF):
        for c in range(HALF):
            table[base + (c + 1) % HALF, base + c] += 1.0
            table[base + (c - 1) % HALF, base + c] += 1.0
            table[c, lanes + base + c] -= 1.0
            table[HALF + c, lanes + base + c] += 1.0
    return np.concatenate([table, table], axis=0).astype(jnp.bfloat16)


def means_table():
    same = np.kron(np.eye(2), np.ones((HALF, HALF))) / HALF
    return np.concatenate([same, same], axis=0).astype(jnp.bfloat16)


def two_parts(value):
    lead = value.astype(jnp.bfloat16)
    trail = (value - lead.astype(F32)).astype(jnp.bfloat16)
    return jnp.concatenate([lead, trail], axis=1)


EARLY = 32
LATE = LEV - EARLY
SENT = LATE + 1
CHUNKS = [(0, 8), (8, 8), (16, 8), (24, 8), (32, 8), (40, 8), (48, 8), (56, 2)]


def substep(source, first, count, forced, active, table):
    rows = count * SLOTS
    at = lambda l, n: source[l * SLOTS : (l + n) * SLOTS, :]
    current = at(first, count)
    if first + count < LEV:
        upper = at(first + 1, count)
    else:
        upper = jnp.concatenate([at(first + 1, count - 1), at(LEV - 1, 1)], axis=0)
    if first > 0:
        lower = at(first - 1, count)
    else:
        lower = jnp.concatenate([at(0, 1), at(0, count - 1)], axis=0)
    mixed = jnp.dot(two_parts(current), table, preferred_element_type=F32)
    side, gap = mixed[:, : 2 * HALF], mixed[:, 2 * HALF :]
    soft = jnp.maximum(gap, 0.0) + jnp.log(1.0 + jnp.exp(-jnp.abs(gap)))
    sign = jnp.where(iota((rows, 2 * HALF), 1) < HALF, 0.05, -0.1)
    updated = 0.5 * current + forced + 0.15 * side + 0.1 * (upper + lower) + sign * soft
    on = jnp.broadcast_to(active, (SLOTS, 2 * HALF))
    return jnp.where(jnp.concatenate([on] * count, axis=0), updated, current)


def spread(quarter, first, count):
    lane = iota((SLOTS, 2 * HALF), 1)
    return jnp.concatenate(
        [
            jnp.take_along_axis(quarter, (lane & HALF) + level, axis=1, mode="promise_in_bounds")
            for level in range(first, first + count)
        ],
        axis=0,
    )


def run_cloud(state, force, table, middle, keep):
    steps = force[:, LEV + 1 : LEV + 2]
    quarter = 0.25 * force[...]
    for first, count in CHUNKS:
        forced = spread(quarter, first, count)
        rows = pl.ds(first * SLOTS, count * SLOTS)
        middle[rows, :] = substep(state, first, count, forced, steps > 0.5, table[...])
    for first, count in CHUNKS:
        forced = spread(quarter, first, count)
        keep(first, count, substep(middle, first, count, forced, steps > 1.5, table[...]))


def tendency_kernel(state, force, table, means, send, middle):
    column = iota((SLOTS, 2 * HALF), 1) & (HALF - 1)
    send[...] = jnp.zeros((SLOTS, 2 * HALF), F32)

    def keep(first, count, stepped):
        change = stepped - state[first * SLOTS : (first + count) * SLOTS, :]
        mean = jnp.dot(two_parts(change), means[...], preferred_element_type=F32)
        total = send[...]
        for i in range(count):
            total = jnp.where(column == first + i, mean[i * SLOTS : (i + 1) * SLOTS, :], total)
        send[...] = total

    run_cloud(state, force, table, middle, keep)


def arrive_kernel(early, late, table, out, held, middle, stepped_at, force, row, origin, done, written):
    last = late[pl.ds(LATE, N_GRP, stride=SENT), :]
    slot = (iota((N_GRP, SLOTS), 1) + 1).astype(F32)
    pick = jnp.where(last[:, LEV : LEV + 1] == slot, 1.0, 0.0).astype(F32)
    group = iota((N_GRP, SLOTS), 0).astype(F32)
    row[...] = jnp.sum(pick * group, axis=0, keepdims=True).astype(jnp.int32)
    copy = pltpu.make_async_copy(row, origin, done)
    copy.start()
    force[...] = dot_t(pick, last)
    copy.wait()
    for j in range(SLOTS):
        g = origin[0, j]
        held[pl.ds(j, EARLY, stride=SLOTS), :] = early[pl.ds(pl.multiple_of(g * EARLY, 8), EARLY), :]
        held[pl.ds(EARLY * SLOTS + j, LATE, stride=SLOTS), :] = late[pl.ds(g * SENT, LATE), :]

    copies = []

    def keep(first, count, stepped):
        rows = pl.ds(first * SLOTS, count * SLOTS)
        stepped_at[rows, :] = stepped
        copies.append(pltpu.make_async_copy(stepped_at.at[rows], out.at[rows], written.at[len(copies)]))
        copies[-1].start()

    run_cloud(held, force, table, middle, keep)
    for copy in copies:
        copy.wait()


def next_kernel(dyn, inner, edge, out):
    me = lax.axis_index("mem")
    behind = lax.rem(me + N_MEM - 1, N_MEM)
    for y in range(ROWS):
        point = iota((POINTS, 2 * HALF), 0)
        left = edge[pl.ds(behind * ROWS + y, 1), :]
        right = edge[pl.ds(me * ROWS + y, 1), :]
        ratio = jnp.where(point == 0, left, jnp.where(point == POINTS - 1, right, inner[y]))
        out[0, y] = dyn[0, y] + 0.2 * ratio[:, :LEV]
        out[1, y] = dyn[1, y] + 0.2 * ratio[:, HALF : HALF + LEV]


def column_kernel(tendency, gathered, out):
    serves = gathered[:, :SLOTS, :].reshape(COLS, 2 * HALF)[:, LEV : LEV + 1]
    column = (iota((COLS, SLOTS), 1) + lax.axis_index("mem") * SLOTS).astype(F32)
    pick = jnp.where(serves == column, 1.0, 0.0).astype(F32)
    mine = dot_t(pick, tendency[...])
    out[0] = mine[:, :LEV]
    out[1] = mine[:, HALF : HALF + LEV]


def call(kernel, shapes, specs, scratch=(), out_specs=None, aliases=None, limit=24):
    many = isinstance(shapes, list)
    out = [jax.ShapeDtypeStruct(s, F32) for s in shapes] if many else jax.ShapeDtypeStruct(shapes, F32)
    return pl.pallas_call(
        kernel,
        out_shape=out,
        in_specs=specs,
        out_specs=out_specs or ([VMEM] * len(shapes) if many else VMEM),
        scratch_shapes=[pltpu.VMEM(s, F32) if isinstance(s, tuple) else s for s in scratch],
        input_output_aliases=aliases or {},
        compiler_params=pltpu.CompilerParams(vmem_limit_bytes=limit * 2**20),
    )


def on_device(dyn_state, wind_speed, mass_weight, crm_state, batch_map, sub_steps, migrate_to):
    lanes = 2 * HALF
    dyn = dyn_state.transpose(0, 2, 3, 1)
    wind = wind_speed.transpose(1, 2, 0)
    state = crm_state.transpose(1, 0, 2).reshape(LEV * SLOTS, lanes)
    batch, steps, moves = (a.reshape(1, SLOTS) for a in (batch_map, sub_steps, migrate_to))
    table = jnp.asarray(np.kron(np.eye(ROWS * POINTS // 4), derivative_table()).astype(np.float32))

    cells = LEV * SLOTS
    dma = pltpu.SemaphoreType.DMA
    ints = pltpu.VMEM((1, SLOTS), jnp.int32)
    weighed, top, end, index, early, late = call(
        first_kernel,
        [(ROWS, POINTS, lanes), (1, POINTS, lanes), (1, POINTS, lanes), (SLOTS, lanes)]
        + [(N_GRP * EARLY, lanes), (N_GRP * SENT, lanes)],
        [HBM] * 9,
        [(cells, lanes), pltpu.SMEM((1, SLOTS), jnp.int32)]
        + [(2, ROWS, POINTS, LEV), (ROWS, POINTS, LEV), (ROWS, POINTS), table.shape, ints, ints, ints]
        + [(N_GRP * EARLY, lanes), (N_GRP * SENT, lanes), dma((9,)), dma((2,))],
        [VMEM] * 4 + [HBM] * 2,
        limit=60,
    )(state, moves, dyn, wind, mass_weight, table, batch, moves, steps)
    up = [(i, (i + 1) % N_GRP) for i in range(N_GRP)]
    down = [(j, i) for i, j in up]
    before = lax.ppermute(end, "grp", up)
    after = lax.ppermute(top, "grp", down)
    early, before, after = lax.optimization_barrier((early, before, after))
    first = lax.all_to_all(early.reshape(N_GRP, EARLY, 1, lanes), "grp", 0, 0, tiled=True)
    inner, payload = call(
        assemble_kernel, [(ROWS, POINTS, lanes), (SLOTS + 2 * ROWS, lanes)], [VMEM] * 3
    )(weighed, before, after)
    gathered = lax.all_gather(payload, "mem", axis=0)
    force, edge, filled = call(
        forcing_kernel,
        [(SLOTS, lanes), (N_MEM * ROWS, lanes), (N_GRP * SENT, lanes)],
        [VMEM] * 3,
    )(gathered, index, late)
    filled, first = lax.optimization_barrier((filled, first))
    second = lax.all_to_all(filled.reshape(N_GRP, SENT, 1, lanes), "grp", 0, 0, tiled=True)
    mix, means = jnp.asarray(neighbours_table()), jnp.asarray(means_table())
    tendency = call(tendency_kernel, (SLOTS, lanes), [VMEM] * 4, [(cells, lanes)])(state, force, mix, means)
    tendencies = lax.all_gather(tendency, "mem", axis=0, tiled=True)
    dyn_next = call(next_kernel, (2, ROWS, POINTS, LEV), [VMEM] * 3)(dyn, inner, edge)
    phys = call(column_kernel, (2, SLOTS, LEV), [VMEM] * 2)(tendencies, gathered)
    new = call(
        arrive_kernel,
        (cells, lanes),
        [VMEM] * 3,
        [(cells, lanes)] * 3
        + [(SLOTS, lanes), ints, pltpu.SMEM((1, SLOTS), jnp.int32), dma, dma((len(CHUNKS),))],
        HBM,
    )(first.reshape(N_GRP * EARLY, lanes), second.reshape(N_GRP * SENT, lanes), mix)
    crm_next = new.reshape(LEV, SLOTS, lanes).transpose(1, 0, 2)
    return (dyn_next.transpose(0, 3, 1, 2), phys.transpose(0, 2, 1), crm_next)


def solution(mesh):
    placed = (
        P(None, None, "grp", "mem"),
        P(None, "grp", "mem"),
        P("grp", "mem"),
        P(("grp", "mem"), None, None),
        P(("grp", "mem")),
        P(("grp", "mem")),
        P(("grp", "mem")),
    )
    return jax.shard_map(
        on_device,
        mesh=mesh,
        in_specs=placed,
        out_specs=(
            P(None, None, "grp", "mem"),
            P(None, None, ("grp", "mem")),
            P(("grp", "mem"), None, None),
        ),
        check_vma=False,
    )
```

```python
import jax
import jax.numpy as jnp
import numpy as np
from jax import lax
from jax.experimental import pallas as pl
from jax.experimental.pallas import tpu as pltpu
from jax.sharding import PartitionSpec as P

NSUB = 2
LEV = 58
HALF = 64
SLOTS = 32
N_GRP = 64
N_MEM = 12
ROWS = 4
POINTS = 32
COLS = SLOTS * N_MEM
HIGH = lax.Precision.HIGHEST
VMEM = pl.BlockSpec(memory_space=pltpu.VMEM)
SMEM = pl.BlockSpec(memory_space=pltpu.SMEM)
HBM = pl.BlockSpec(memory_space=pltpu.HBM)
F32 = jnp.float32


def derivative_table():
    nodes = np.array([-1.0, -1.0 / np.sqrt(5.0), 1.0 / np.sqrt(5.0), 1.0])
    table = np.zeros((4, 4))
    for i in range(4):
        for j in range(4):
            if i == j:
                table[i, j] = sum(1.0 / (nodes[j] - nodes[k]) for k in range(4) if k != j)
            else:
                top = np.prod([nodes[i] - nodes[k] for k in range(4) if k not in (i, j)])
                low = np.prod([nodes[j] - nodes[k] for k in range(4) if k != j])
                table[i, j] = top / low
    return table.astype(np.float32)


def iota(shape, dim):
    return lax.broadcasted_iota(jnp.int32, shape, dim)


def dot(a, b):
    return jnp.dot(a, b, precision=HIGH, preferred_element_type=F32)


def dot_t(a, b):
    return lax.dot_general(a, b, (((0,), (0,)), ((), ())), precision=HIGH, preferred_element_type=F32)


def to_column(row):
    n = row.shape[1]
    return jnp.sum(jnp.where(iota((n, n), 0) == iota((n, n), 1), row, 0.0), axis=1, keepdims=True)


def both_kinds(heat, moist):
    gap = jnp.zeros((heat.shape[0], HALF - LEV), F32)
    return jnp.concatenate([heat, gap, moist, gap], axis=1)


def bucket_kernel(migrate, state, batch, moves, steps, early, late, index):
    new = moves[...]
    group = jnp.floor((new.astype(F32) + 0.5) * (1.0 / COLS))
    place = (new & (SLOTS - 1)).astype(F32) + 1.0
    lane = iota((SLOTS, 2 * HALF), 1)
    columns = jnp.zeros((SLOTS, 2 * HALF), F32)
    for i, row in enumerate((batch[...].astype(F32), place, steps[...].astype(F32), group)):
        columns = jnp.where(lane == i, to_column(row), columns)
    index[...] = columns
    for s in range(SLOTS):
        group = lax.div(migrate[s], COLS)
        early[pl.ds(group * EARLY, EARLY), :] = state[pl.ds(s, EARLY, stride=SLOTS), :]
        late[pl.ds(group * SENT, LATE), :] = state[pl.ds(EARLY * SLOTS + s, LATE, stride=SLOTS), :]


def weigh_kernel(dyn_at, wind_at, mass_at, table_at, batch_at, out, top, end, dyn, wind, mass, table, batch, done):
    pairs = [(dyn_at, dyn), (wind_at, wind), (mass_at, mass), (table_at, table), (batch_at, batch)]
    copies = [pltpu.make_async_copy(a, b, done.at[i]) for i, (a, b) in enumerate(pairs)]
    for copy in copies:
        copy.start()
    for copy in copies:
        copy.wait()
    field = both_kinds(dyn[0].reshape(ROWS * POINTS, LEV), dyn[1].reshape(ROWS * POINTS, LEV))
    blow = wind[...].reshape(ROWS * POINTS, LEV)
    slope = dot(table[...], field)
    column = jnp.concatenate([to_column(mass[y : y + 1, :]) for y in range(ROWS)], axis=0)
    weighed = column * (-both_kinds(blow, blow) * slope)
    lane = iota((ROWS * POINTS, 2 * HALF), 1)
    serves = jnp.concatenate([to_column(batch[...].astype(F32))] * ROWS, axis=0)
    spare = jnp.where(lane == LEV, column, serves)
    weighed = jnp.where((lane == LEV) | (lane == LEV + 1), spare, weighed)
    weighed = weighed.reshape(ROWS, POINTS, 2 * HALF)
    out[...] = weighed
    top[0] = weighed[0]
    end[0] = weighed[ROWS - 1]


def assemble_kernel(own, before, after, inner, payload):
    rows = [own[0] + before[0], own[1], own[2], own[3] + after[0]]
    point = iota((POINTS, 2 * HALF), 0)
    means, edges = [], []
    for y, row in enumerate(rows):
        opening = (point % 4 == 0) & (point > 0)
        closing = (point % 4 == 3) & (point < POINTS - 1)
        full = (
            row
            + jnp.where(opening, pltpu.roll(row, 1, 0), 0.0)
            + jnp.where(closing, pltpu.roll(row, POINTS - 1, 0), 0.0)
        )
        ratio = full / full[:, LEV : LEV + 1]
        inner[y] = ratio
        means.append(jnp.where((point == 0) | (point == POINTS - 1), 0.0, ratio))
        edges.append(row)
    col, pt = iota((SLOTS, ROWS * POINTS), 0), iota((SLOTS, ROWS * POINTS), 1)
    inside = (col // 16 == pt // (2 * POINTS)) & (col % 16 == (pt % POINTS) // 2)
    average = jnp.where(inside, 0.25, 0.0).astype(F32)
    forcing = dot(average, jnp.concatenate(means, axis=0))
    left = [row[0:1] for row in edges]
    right = [row[POINTS - 1 : POINTS] for row in edges]
    lane = iota((SLOTS, 2 * HALF), 1)
    forcing = jnp.where(lane == LEV, own[0][:, LEV + 1 : LEV + 2], forcing)
    payload[...] = jnp.concatenate([forcing] + left + right, axis=0)


def forcing_kernel(gathered, index, late, force, edge, filled):
    rows = []
    for d in range(N_MEM):
        right = gathered[d, SLOTS + ROWS : SLOTS + 2 * ROWS, :]
        left = gathered[(d + 1) % N_MEM, SLOTS : SLOTS + ROWS, :]
        both = right + left
        rows.append(both / both[:, LEV : LEV + 1])
    joined = jnp.concatenate(rows, axis=0)
    edge[...] = joined
    columns = gathered[:, :SLOTS, :].reshape(COLS, 2 * HALF)
    slot = index[:, 0:1].astype(jnp.int32)
    pick = jnp.where(iota((SLOTS, COLS), 1) == slot, 1.0, 0.0).astype(F32)
    e = iota((SLOTS, N_MEM * ROWS), 1)
    dev, half = e // ROWS, (e % ROWS) // 2
    ahead = jnp.where(dev == N_MEM - 1, 0, dev + 1)
    last = slot == dev * SLOTS + half * 16 + 15
    first = slot == ahead * SLOTS + half * 16
    pick_edge = jnp.where(last, 0.25, 0.0) + jnp.where(first, 0.25, 0.0)
    forced = dot(pick, columns) + dot(pick_edge, joined)
    lane = iota((SLOTS, 2 * HALF), 1)
    forced = jnp.where(lane == LEV, index[:, 1:2], jnp.where(lane == LEV + 1, index[:, 2:3], forced))
    force[...] = forced
    goes = jnp.where(iota((SLOTS, N_GRP), 1) == index[:, 3:4].astype(jnp.int32), 1.0, 0.0).astype(F32)
    filled[...] = late[...]
    filled[pl.ds(LATE, N_GRP, stride=SENT), :] = dot_t(goes, forced)


def neighbours_table():
    lanes = 2 * HALF
    table = np.zeros((lanes, 2 * lanes))
    for base in (0, HALF):
        for c in range(HALF):
            table[base + (c + 1) % HALF, base + c] += 1.0
            table[base + (c - 1) % HALF, base + c] += 1.0
            table[c, lanes + base + c] -= 1.0
            table[HALF + c, lanes + base + c] += 1.0
    return np.concatenate([table, table], axis=0).astype(jnp.bfloat16)


def means_table():
    same = np.kron(np.eye(2), np.ones((HALF, HALF))) / HALF
    return np.concatenate([same, same], axis=0).astype(jnp.bfloat16)


def two_parts(value):
    lead = value.astype(jnp.bfloat16)
    trail = (value - lead.astype(F32)).astype(jnp.bfloat16)
    return jnp.concatenate([lead, trail], axis=1)


EARLY = 34
LATE = LEV - EARLY
SENT = LATE + 1
CHUNKS = [(0, 8), (8, 8), (16, 8), (24, 8), (32, 8), (40, 8), (48, 8), (56, 2)]


def substep(source, first, count, forced, active, table):
    rows = count * SLOTS
    at = lambda l, n: source[l * SLOTS : (l + n) * SLOTS, :]
    current = at(first, count)
    if first + count < LEV:
        upper = at(first + 1, count)
    else:
        upper = jnp.concatenate([at(first + 1, count - 1), at(LEV - 1, 1)], axis=0)
    if first > 0:
        lower = at(first - 1, count)
    else:
        lower = jnp.concatenate([at(0, 1), at(0, count - 1)], axis=0)
    mixed = jnp.dot(two_parts(current), table, preferred_element_type=F32)
    side, gap = mixed[:, : 2 * HALF], mixed[:, 2 * HALF :]
    soft = jnp.maximum(gap, 0.0) + jnp.log(1.0 + jnp.exp(-jnp.abs(gap)))
    sign = jnp.where(iota((rows, 2 * HALF), 1) < HALF, 0.05, -0.1)
    updated = 0.5 * current + forced + 0.15 * side + 0.1 * (upper + lower) + sign * soft
    on = jnp.broadcast_to(active, (SLOTS, 2 * HALF))
    return jnp.where(jnp.concatenate([on] * count, axis=0), updated, current)


def spread(quarter, first, count):
    lane = iota((SLOTS, 2 * HALF), 1)
    return jnp.concatenate(
        [
            jnp.take_along_axis(quarter, (lane & HALF) + level, axis=1, mode="promise_in_bounds")
            for level in range(first, first + count)
        ],
        axis=0,
    )


def run_cloud(state, force, table, middle, keep):
    steps = force[:, LEV + 1 : LEV + 2]
    quarter = 0.25 * force[...]
    for first, count in CHUNKS:
        forced = spread(quarter, first, count)
        rows = pl.ds(first * SLOTS, count * SLOTS)
        middle[rows, :] = substep(state, first, count, forced, steps > 0.5, table[...])
    for first, count in CHUNKS:
        forced = spread(quarter, first, count)
        keep(first, count, substep(middle, first, count, forced, steps > 1.5, table[...]))


def tendency_kernel(state, force, table, means, send, middle):
    column = iota((SLOTS, 2 * HALF), 1) & (HALF - 1)
    send[...] = jnp.zeros((SLOTS, 2 * HALF), F32)

    def keep(first, count, stepped):
        change = stepped - state[first * SLOTS : (first + count) * SLOTS, :]
        mean = jnp.dot(two_parts(change), means[...], preferred_element_type=F32)
        total = send[...]
        for i in range(count):
            total = jnp.where(column == first + i, mean[i * SLOTS : (i + 1) * SLOTS, :], total)
        send[...] = total

    run_cloud(state, force, table, middle, keep)


def arrive_kernel(early, late, table, out, held, middle, stepped_at, force, row, origin, done, written):
    last = late[pl.ds(LATE, N_GRP, stride=SENT), :]
    slot = (iota((N_GRP, SLOTS), 1) + 1).astype(F32)
    pick = jnp.where(last[:, LEV : LEV + 1] == slot, 1.0, 0.0).astype(F32)
    group = iota((N_GRP, SLOTS), 0).astype(F32)
    row[...] = jnp.sum(pick * group, axis=0, keepdims=True).astype(jnp.int32)
    copy = pltpu.make_async_copy(row, origin, done)
    copy.start()
    force[...] = dot_t(pick, last)
    copy.wait()
    for j in range(SLOTS):
        g = origin[0, j]
        held[pl.ds(j, EARLY, stride=SLOTS), :] = early[pl.ds(g * EARLY, EARLY), :]
        held[pl.ds(EARLY * SLOTS + j, LATE, stride=SLOTS), :] = late[pl.ds(g * SENT, LATE), :]

    copies = []

    def keep(first, count, stepped):
        rows = pl.ds(first * SLOTS, count * SLOTS)
        stepped_at[rows, :] = stepped
        copies.append(pltpu.make_async_copy(stepped_at.at[rows], out.at[rows], written.at[len(copies)]))
        copies[-1].start()

    run_cloud(held, force, table, middle, keep)
    for copy in copies:
        copy.wait()


def finish_kernel(tendency, gathered, dyn, inner, edge, phys, out):
    me = lax.axis_index("mem")
    serves = gathered[:, :SLOTS, :].reshape(COLS, 2 * HALF)[:, LEV : LEV + 1]
    column = (iota((COLS, SLOTS), 1) + me * SLOTS).astype(F32)
    pick = jnp.where(serves == column, 1.0, 0.0).astype(jnp.bfloat16)
    parts = lax.dot_general(
        pick, two_parts(tendency[...]), (((0,), (0,)), ((), ())), preferred_element_type=F32
    )
    mine = parts[:, : 2 * HALF] + parts[:, 2 * HALF :]
    phys[0] = mine[:, :LEV]
    phys[1] = mine[:, HALF : HALF + LEV]
    behind = lax.rem(me + N_MEM - 1, N_MEM)
    for y in range(ROWS):
        point = iota((POINTS, 2 * HALF), 0)
        left = edge[pl.ds(behind * ROWS + y, 1), :]
        right = edge[pl.ds(me * ROWS + y, 1), :]
        ratio = jnp.where(point == 0, left, jnp.where(point == POINTS - 1, right, inner[y]))
        out[0, y] = dyn[0, y] + 0.2 * ratio[:, :LEV]
        out[1, y] = dyn[1, y] + 0.2 * ratio[:, HALF : HALF + LEV]


def call(kernel, shapes, specs, scratch=(), out_specs=None, aliases=None, limit=24):
    many = isinstance(shapes, list)
    out = [jax.ShapeDtypeStruct(s, F32) for s in shapes] if many else jax.ShapeDtypeStruct(shapes, F32)
    return pl.pallas_call(
        kernel,
        out_shape=out,
        in_specs=specs,
        out_specs=out_specs or ([VMEM] * len(shapes) if many else VMEM),
        scratch_shapes=[pltpu.VMEM(s, F32) if isinstance(s, tuple) else s for s in scratch],
        input_output_aliases=aliases or {},
        compiler_params=pltpu.CompilerParams(vmem_limit_bytes=limit * 2**20),
    )


def on_device(dyn_state, wind_speed, mass_weight, crm_state, batch_map, sub_steps, migrate_to):
    lanes = 2 * HALF
    dyn = dyn_state.transpose(0, 2, 3, 1)
    wind = wind_speed.transpose(1, 2, 0)
    state = crm_state.transpose(1, 0, 2).reshape(LEV * SLOTS, lanes)
    batch, steps, moves = (a.reshape(1, SLOTS) for a in (batch_map, sub_steps, migrate_to))
    table = jnp.asarray(np.kron(np.eye(ROWS * POINTS // 4), derivative_table()).astype(np.float32))

    cells = LEV * SLOTS
    dma = pltpu.SemaphoreType.DMA
    ints = pltpu.VMEM((1, SLOTS), jnp.int32)
    weighed, top, end = call(
        weigh_kernel,
        [(ROWS, POINTS, lanes), (1, POINTS, lanes), (1, POINTS, lanes)],
        [HBM] * 5,
        [(2, ROWS, POINTS, LEV), (ROWS, POINTS, LEV), (ROWS, POINTS), table.shape, ints, dma((5,))],
        limit=60,
    )(dyn, wind, mass_weight, table, batch)
    weighed, batch_later = lax.optimization_barrier((weighed, batch))
    early, late, index = call(
        bucket_kernel, [(N_GRP * EARLY, lanes), (N_GRP * SENT, lanes), (SLOTS, lanes)], [SMEM] + [VMEM] * 4
    )(migrate_to, state, batch_later, moves, steps)
    up = [(i, (i + 1) % N_GRP) for i in range(N_GRP)]
    down = [(j, i) for i, j in up]
    before = lax.ppermute(end, "grp", up)
    after = lax.ppermute(top, "grp", down)
    early, before, after = lax.optimization_barrier((early, before, after))
    first = lax.all_to_all(early.reshape(N_GRP, EARLY, 1, lanes), "grp", 0, 0, tiled=True)
    inner, payload = call(
        assemble_kernel, [(ROWS, POINTS, lanes), (SLOTS + 2 * ROWS, lanes)], [VMEM] * 3
    )(weighed, before, after)
    gathered = lax.all_gather(payload, "mem", axis=0)
    force, edge, filled = call(
        forcing_kernel,
        [(SLOTS, lanes), (N_MEM * ROWS, lanes), (N_GRP * SENT, lanes)],
        [VMEM] * 3,
    )(gathered, index, late)
    filled, first = lax.optimization_barrier((filled, first))
    second = lax.all_to_all(filled.reshape(N_GRP, SENT, 1, lanes), "grp", 0, 0, tiled=True)
    mix, means = jnp.asarray(neighbours_table()), jnp.asarray(means_table())
    tendency = call(tendency_kernel, (SLOTS, lanes), [VMEM] * 4, [(cells, lanes)])(state, force, mix, means)
    tendencies = lax.all_gather(tendency, "mem", axis=0, tiled=True)
    phys, dyn_next = call(
        finish_kernel, [(2, SLOTS, LEV), (2, ROWS, POINTS, LEV)], [VMEM] * 5
    )(tendencies, gathered, dyn, inner, edge)
    new = call(
        arrive_kernel,
        (cells, lanes),
        [VMEM] * 3,
        [(cells, lanes)] * 3
        + [(SLOTS, lanes), ints, pltpu.SMEM((1, SLOTS), jnp.int32), dma, dma((len(CHUNKS),))],
        HBM,
    )(first.reshape(N_GRP * EARLY, lanes), second.reshape(N_GRP * SENT, lanes), mix)
    crm_next = new.reshape(LEV, SLOTS, lanes).transpose(1, 0, 2)
    return (dyn_next.transpose(0, 3, 1, 2), phys.transpose(0, 2, 1), crm_next)


def solution(mesh):
    placed = (
        P(None, None, "grp", "mem"),
        P(None, "grp", "mem"),
        P("grp", "mem"),
        P(("grp", "mem"), None, None),
        P(("grp", "mem")),
        P(("grp", "mem")),
        P(("grp", "mem")),
    )
    return jax.shard_map(
        on_device,
        mesh=mesh,
        in_specs=placed,
        out_specs=(
            P(None, None, "grp", "mem"),
            P(None, None, ("grp", "mem")),
            P(("grp", "mem"), None, None),
        ),
        check_vma=False,
    )
```

```python
import jax
import jax.numpy as jnp
import numpy as np
from jax import lax
from jax.experimental import pallas as pl
from jax.experimental.pallas import tpu as pltpu
from jax.sharding import PartitionSpec as P

NSUB = 2
LEV = 58
HALF = 64
SLOTS = 32
N_GRP = 64
N_MEM = 12
ROWS = 4
POINTS = 32
COLS = SLOTS * N_MEM
HIGH = lax.Precision.HIGHEST
VMEM = pl.BlockSpec(memory_space=pltpu.VMEM)
SMEM = pl.BlockSpec(memory_space=pltpu.SMEM)
HBM = pl.BlockSpec(memory_space=pltpu.HBM)
F32 = jnp.float32


def derivative_table():
    nodes = np.array([-1.0, -1.0 / np.sqrt(5.0), 1.0 / np.sqrt(5.0), 1.0])
    table = np.zeros((4, 4))
    for i in range(4):
        for j in range(4):
            if i == j:
                table[i, j] = sum(1.0 / (nodes[j] - nodes[k]) for k in range(4) if k != j)
            else:
                top = np.prod([nodes[i] - nodes[k] for k in range(4) if k not in (i, j)])
                low = np.prod([nodes[j] - nodes[k] for k in range(4) if k != j])
                table[i, j] = top / low
    return table.astype(np.float32)


def iota(shape, dim):
    return lax.broadcasted_iota(jnp.int32, shape, dim)


def dot(a, b):
    return jnp.dot(a, b, precision=HIGH, preferred_element_type=F32)


def dot_t(a, b):
    return lax.dot_general(a, b, (((0,), (0,)), ((), ())), precision=HIGH, preferred_element_type=F32)


def to_column(row):
    n = row.shape[1]
    return jnp.sum(jnp.where(iota((n, n), 0) == iota((n, n), 1), row, 0.0), axis=1, keepdims=True)


def both_kinds(heat, moist):
    gap = jnp.zeros((heat.shape[0], HALF - LEV), F32)
    return jnp.concatenate([heat, gap, moist, gap], axis=1)


def bucket_kernel(migrate, state, batch, moves, steps, early, late, index):
    new = moves[...]
    group = jnp.floor((new.astype(F32) + 0.5) * (1.0 / COLS))
    place = (new & (SLOTS - 1)).astype(F32) + 1.0
    lane = iota((SLOTS, 2 * HALF), 1)
    columns = jnp.zeros((SLOTS, 2 * HALF), F32)
    for i, row in enumerate((batch[...].astype(F32), place, steps[...].astype(F32), group)):
        columns = jnp.where(lane == i, to_column(row), columns)
    index[...] = columns
    for s in range(SLOTS):
        group = lax.div(migrate[s], COLS)
        early[pl.ds(pl.multiple_of(group * EARLY, 8), EARLY), :] = state[pl.ds(s, EARLY, stride=SLOTS), :]
        late[pl.ds(group * SENT, LATE), :] = state[pl.ds(EARLY * SLOTS + s, LATE, stride=SLOTS), :]


def weigh_kernel(dyn_at, wind_at, mass_at, table_at, batch_at, out, top, end, dyn, wind, mass, table, batch, done):
    pairs = [(dyn_at, dyn), (wind_at, wind), (mass_at, mass), (table_at, table), (batch_at, batch)]
    copies = [pltpu.make_async_copy(a, b, done.at[i]) for i, (a, b) in enumerate(pairs)]
    for copy in copies:
        copy.start()
    for copy in copies:
        copy.wait()
    field = both_kinds(dyn[0].reshape(ROWS * POINTS, LEV), dyn[1].reshape(ROWS * POINTS, LEV))
    blow = wind[...].reshape(ROWS * POINTS, LEV)
    slope = dot(table[...], field)
    column = jnp.concatenate([to_column(mass[y : y + 1, :]) for y in range(ROWS)], axis=0)
    weighed = column * (-both_kinds(blow, blow) * slope)
    lane = iota((ROWS * POINTS, 2 * HALF), 1)
    serves = jnp.concatenate([to_column(batch[...].astype(F32))] * ROWS, axis=0)
    spare = jnp.where(lane == LEV, column, serves)
    weighed = jnp.where((lane == LEV) | (lane == LEV + 1), spare, weighed)
    weighed = weighed.reshape(ROWS, POINTS, 2 * HALF)
    out[...] = weighed
    top[0] = weighed[0]
    end[0] = weighed[ROWS - 1]


def assemble_kernel(own, before, after, inner, payload):
    rows = [own[0] + before[0], own[1], own[2], own[3] + after[0]]
    point = iota((POINTS, 2 * HALF), 0)
    means, edges = [], []
    for y, row in enumerate(rows):
        opening = (point % 4 == 0) & (point > 0)
        closing = (point % 4 == 3) & (point < POINTS - 1)
        full = (
            row
            + jnp.where(opening, pltpu.roll(row, 1, 0), 0.0)
            + jnp.where(closing, pltpu.roll(row, POINTS - 1, 0), 0.0)
        )
        ratio = full / full[:, LEV : LEV + 1]
        inner[y] = ratio
        means.append(jnp.where((point == 0) | (point == POINTS - 1), 0.0, ratio))
        edges.append(row)
    col, pt = iota((SLOTS, ROWS * POINTS), 0), iota((SLOTS, ROWS * POINTS), 1)
    inside = (col // 16 == pt // (2 * POINTS)) & (col % 16 == (pt % POINTS) // 2)
    average = jnp.where(inside, 0.25, 0.0).astype(F32)
    forcing = dot(average, jnp.concatenate(means, axis=0))
    left = [row[0:1] for row in edges]
    right = [row[POINTS - 1 : POINTS] for row in edges]
    lane = iota((SLOTS, 2 * HALF), 1)
    forcing = jnp.where(lane == LEV, own[0][:, LEV + 1 : LEV + 2], forcing)
    payload[...] = jnp.concatenate([forcing] + left + right, axis=0)


def forcing_kernel(gathered, index, late, force, edge, filled):
    rows = []
    for d in range(N_MEM):
        right = gathered[d, SLOTS + ROWS : SLOTS + 2 * ROWS, :]
        left = gathered[(d + 1) % N_MEM, SLOTS : SLOTS + ROWS, :]
        both = right + left
        rows.append(both / both[:, LEV : LEV + 1])
    joined = jnp.concatenate(rows, axis=0)
    edge[...] = joined
    columns = gathered[:, :SLOTS, :].reshape(COLS, 2 * HALF)
    slot = index[:, 0:1].astype(jnp.int32)
    pick = jnp.where(iota((SLOTS, COLS), 1) == slot, 1.0, 0.0).astype(F32)
    e = iota((SLOTS, N_MEM * ROWS), 1)
    dev, half = e // ROWS, (e % ROWS) // 2
    ahead = jnp.where(dev == N_MEM - 1, 0, dev + 1)
    last = slot == dev * SLOTS + half * 16 + 15
    first = slot == ahead * SLOTS + half * 16
    pick_edge = jnp.where(last, 0.25, 0.0) + jnp.where(first, 0.25, 0.0)
    forced = dot(pick, columns) + dot(pick_edge, joined)
    lane = iota((SLOTS, 2 * HALF), 1)
    forced = jnp.where(lane == LEV, index[:, 1:2], jnp.where(lane == LEV + 1, index[:, 2:3], forced))
    force[...] = forced
    goes = jnp.where(iota((SLOTS, N_GRP), 1) == index[:, 3:4].astype(jnp.int32), 1.0, 0.0).astype(F32)
    filled[...] = late[...]
    filled[pl.ds(LATE, N_GRP, stride=SENT), :] = dot_t(goes, forced)


def neighbours_table():
    lanes = 2 * HALF
    table = np.zeros((lanes, 2 * lanes))
    for base in (0, HALF):
        for c in range(HALF):
            table[base + (c + 1) % HALF, base + c] += 1.0
            table[base + (c - 1) % HALF, base + c] += 1.0
            table[c, lanes + base + c] -= 1.0
            table[HALF + c, lanes + base + c] += 1.0
    return np.concatenate([table, table], axis=0).astype(jnp.bfloat16)


def means_table():
    same = np.kron(np.eye(2), np.ones((HALF, HALF))) / HALF
    return np.concatenate([same, same], axis=0).astype(jnp.bfloat16)


def two_parts(value):
    lead = value.astype(jnp.bfloat16)
    trail = (value - lead.astype(F32)).astype(jnp.bfloat16)
    return jnp.concatenate([lead, trail], axis=1)


EARLY = 32
LATE = LEV - EARLY
SENT = LATE + 1
CHUNKS = [(0, 8), (8, 8), (16, 8), (24, 8), (32, 8), (40, 8), (48, 8), (56, 2)]


def substep(source, first, count, forced, active, table):
    rows = count * SLOTS
    at = lambda l, n: source[l * SLOTS : (l + n) * SLOTS, :]
    current = at(first, count)
    if first + count < LEV:
        upper = at(first + 1, count)
    else:
        upper = jnp.concatenate([at(first + 1, count - 1), at(LEV - 1, 1)], axis=0)
    if first > 0:
        lower = at(first - 1, count)
    else:
        lower = jnp.concatenate([at(0, 1), at(0, count - 1)], axis=0)
    mixed = jnp.dot(two_parts(current), table, preferred_element_type=F32)
    side, gap = mixed[:, : 2 * HALF], mixed[:, 2 * HALF :]
    soft = jnp.maximum(gap, 0.0) + jnp.log(1.0 + jnp.exp(-jnp.abs(gap)))
    sign = jnp.where(iota((rows, 2 * HALF), 1) < HALF, 0.05, -0.1)
    updated = 0.5 * current + forced + 0.15 * side + 0.1 * (upper + lower) + sign * soft
    on = jnp.broadcast_to(active, (SLOTS, 2 * HALF))
    return jnp.where(jnp.concatenate([on] * count, axis=0), updated, current)


def spread(quarter, first, count):
    lane = iota((SLOTS, 2 * HALF), 1)
    return jnp.concatenate(
        [
            jnp.take_along_axis(quarter, (lane & HALF) + level, axis=1, mode="promise_in_bounds")
            for level in range(first, first + count)
        ],
        axis=0,
    )


def run_cloud(state, force, table, middle, keep):
    steps = force[:, LEV + 1 : LEV + 2]
    quarter = 0.25 * force[...]
    for first, count in CHUNKS:
        forced = spread(quarter, first, count)
        rows = pl.ds(first * SLOTS, count * SLOTS)
        middle[rows, :] = substep(state, first, count, forced, steps > 0.5, table[...])
    for first, count in CHUNKS:
        forced = spread(quarter, first, count)
        keep(first, count, substep(middle, first, count, forced, steps > 1.5, table[...]))


def tendency_kernel(state, force, table, means, send, middle):
    column = iota((SLOTS, 2 * HALF), 1) & (HALF - 1)
    send[...] = jnp.zeros((SLOTS, 2 * HALF), F32)

    def keep(first, count, stepped):
        change = stepped - state[first * SLOTS : (first + count) * SLOTS, :]
        mean = jnp.dot(two_parts(change), means[...], preferred_element_type=F32)
        total = send[...]
        for i in range(count):
            total = jnp.where(column == first + i, mean[i * SLOTS : (i + 1) * SLOTS, :], total)
        send[...] = total

    run_cloud(state, force, table, middle, keep)


def arrive_kernel(early, late, table, out, held, middle, stepped_at, force, row, origin, done, written):
    last = late[pl.ds(LATE, N_GRP, stride=SENT), :]
    slot = (iota((N_GRP, SLOTS), 1) + 1).astype(F32)
    pick = jnp.where(last[:, LEV : LEV + 1] == slot, 1.0, 0.0).astype(F32)
    group = iota((N_GRP, SLOTS), 0).astype(F32)
    row[...] = jnp.sum(pick * group, axis=0, keepdims=True).astype(jnp.int32)
    copy = pltpu.make_async_copy(row, origin, done)
    copy.start()
    force[...] = dot_t(pick, last)
    copy.wait()
    for j in range(SLOTS):
        g = origin[0, j]
        held[pl.ds(j, EARLY, stride=SLOTS), :] = early[pl.ds(pl.multiple_of(g * EARLY, 8), EARLY), :]
        held[pl.ds(EARLY * SLOTS + j, LATE, stride=SLOTS), :] = late[pl.ds(g * SENT, LATE), :]

    copies = []

    def keep(first, count, stepped):
        rows = pl.ds(first * SLOTS, count * SLOTS)
        stepped_at[rows, :] = stepped
        copies.append(pltpu.make_async_copy(stepped_at.at[rows], out.at[rows], written.at[len(copies)]))
        copies[-1].start()

    run_cloud(held, force, table, middle, keep)
    for copy in copies:
        copy.wait()


def finish_kernel(tendency, gathered, dyn, inner, edge, phys, out):
    me = lax.axis_index("mem")
    serves = gathered[:, :SLOTS, :].reshape(COLS, 2 * HALF)[:, LEV : LEV + 1]
    column = (iota((COLS, SLOTS), 1) + me * SLOTS).astype(F32)
    pick = jnp.where(serves == column, 1.0, 0.0).astype(jnp.bfloat16)
    parts = lax.dot_general(
        pick, two_parts(tendency[...]), (((0,), (0,)), ((), ())), preferred_element_type=F32
    )
    mine = parts[:, : 2 * HALF] + parts[:, 2 * HALF :]
    phys[0] = mine[:, :LEV]
    phys[1] = mine[:, HALF : HALF + LEV]
    behind = lax.rem(me + N_MEM - 1, N_MEM)
    for y in range(ROWS):
        point = iota((POINTS, 2 * HALF), 0)
        left = edge[pl.ds(behind * ROWS + y, 1), :]
        right = edge[pl.ds(me * ROWS + y, 1), :]
        ratio = jnp.where(point == 0, left, jnp.where(point == POINTS - 1, right, inner[y]))
        out[0, y] = dyn[0, y] + 0.2 * ratio[:, :LEV]
        out[1, y] = dyn[1, y] + 0.2 * ratio[:, HALF : HALF + LEV]


def call(kernel, shapes, specs, scratch=(), out_specs=None, aliases=None, limit=24):
    many = isinstance(shapes, list)
    out = [jax.ShapeDtypeStruct(s, F32) for s in shapes] if many else jax.ShapeDtypeStruct(shapes, F32)
    return pl.pallas_call(
        kernel,
        out_shape=out,
        in_specs=specs,
        out_specs=out_specs or ([VMEM] * len(shapes) if many else VMEM),
        scratch_shapes=[pltpu.VMEM(s, F32) if isinstance(s, tuple) else s for s in scratch],
        input_output_aliases=aliases or {},
        compiler_params=pltpu.CompilerParams(vmem_limit_bytes=limit * 2**20),
    )


def on_device(dyn_state, wind_speed, mass_weight, crm_state, batch_map, sub_steps, migrate_to):
    lanes = 2 * HALF
    dyn = dyn_state.transpose(0, 2, 3, 1)
    wind = wind_speed.transpose(1, 2, 0)
    state = crm_state.transpose(1, 0, 2).reshape(LEV * SLOTS, lanes)
    batch, steps, moves = (a.reshape(1, SLOTS) for a in (batch_map, sub_steps, migrate_to))
    table = jnp.asarray(np.kron(np.eye(ROWS * POINTS // 4), derivative_table()).astype(np.float32))

    cells = LEV * SLOTS
    dma = pltpu.SemaphoreType.DMA
    ints = pltpu.VMEM((1, SLOTS), jnp.int32)
    weighed, top, end = call(
        weigh_kernel,
        [(ROWS, POINTS, lanes), (1, POINTS, lanes), (1, POINTS, lanes)],
        [HBM] * 5,
        [(2, ROWS, POINTS, LEV), (ROWS, POINTS, LEV), (ROWS, POINTS), table.shape, ints, dma((5,))],
        limit=60,
    )(dyn, wind, mass_weight, table, batch)
    weighed, batch_later = lax.optimization_barrier((weighed, batch))
    early, late, index = call(
        bucket_kernel, [(N_GRP * EARLY, lanes), (N_GRP * SENT, lanes), (SLOTS, lanes)], [SMEM] + [VMEM] * 4
    )(migrate_to, state, batch_later, moves, steps)
    up = [(i, (i + 1) % N_GRP) for i in range(N_GRP)]
    down = [(j, i) for i, j in up]
    before = lax.ppermute(end, "grp", up)
    after = lax.ppermute(top, "grp", down)
    early, before, after = lax.optimization_barrier((early, before, after))
    first = lax.all_to_all(early.reshape(N_GRP, EARLY, 1, lanes), "grp", 0, 0, tiled=True)
    inner, payload = call(
        assemble_kernel, [(ROWS, POINTS, lanes), (SLOTS + 2 * ROWS, lanes)], [VMEM] * 3
    )(weighed, before, after)
    gathered = lax.all_gather(payload, "mem", axis=0)
    force, edge, filled = call(
        forcing_kernel,
        [(SLOTS, lanes), (N_MEM * ROWS, lanes), (N_GRP * SENT, lanes)],
        [VMEM] * 3,
    )(gathered, index, late)
    filled, first = lax.optimization_barrier((filled, first))
    second = lax.all_to_all(filled.reshape(N_GRP, SENT, 1, lanes), "grp", 0, 0, tiled=True)
    mix, means = jnp.asarray(neighbours_table()), jnp.asarray(means_table())
    tendency = call(tendency_kernel, (SLOTS, lanes), [VMEM] * 4, [(cells, lanes)])(state, force, mix, means)
    tendencies = lax.all_gather(tendency, "mem", axis=0, tiled=True)
    phys, dyn_next = call(
        finish_kernel, [(2, SLOTS, LEV), (2, ROWS, POINTS, LEV)], [VMEM] * 5
    )(tendencies, gathered, dyn, inner, edge)
    new = call(
        arrive_kernel,
        (cells, lanes),
        [VMEM] * 3,
        [(cells, lanes)] * 3
        + [(SLOTS, lanes), ints, pltpu.SMEM((1, SLOTS), jnp.int32), dma, dma((len(CHUNKS),))],
        HBM,
    )(first.reshape(N_GRP * EARLY, lanes), second.reshape(N_GRP * SENT, lanes), mix)
    crm_next = new.reshape(LEV, SLOTS, lanes).transpose(1, 0, 2)
    return (dyn_next.transpose(0, 3, 1, 2), phys.transpose(0, 2, 1), crm_next)


def solution(mesh):
    placed = (
        P(None, None, "grp", "mem"),
        P(None, "grp", "mem"),
        P("grp", "mem"),
        P(("grp", "mem"), None, None),
        P(("grp", "mem")),
        P(("grp", "mem")),
        P(("grp", "mem")),
    )
    return jax.shard_map(
        on_device,
        mesh=mesh,
        in_specs=placed,
        out_specs=(
            P(None, None, "grp", "mem"),
            P(None, None, ("grp", "mem")),
            P(("grp", "mem"), None, None),
        ),
        check_vma=False,
    )
```
